128 devices in a mesh: tm: 4 (over z), space: 8 (over y, x_lo), clip: 4 (over x_hi, core).
Axes of the slice: x: 4 (x_hi: 2, x_lo: 2; x = x_hi * 2 + x_lo), y: 4, z: 4, core: 2. Of those that a mesh axis runs over, the one named last changes fastest.
Arguments:
- activations: bfloat16 [96, 256, 1408], P(('clip', 'tm'), 'space'), parts along dimension 0, may hold values from -200 to 200
- attn_gain: float32 [1408], replicated, may hold values from 0.5 to 2
- attn_shift: float32 [1408], replicated, may hold values from -3 to 3
- w_qkv: bfloat16 [1408, 4224], replicated, may hold values from -4 to 4
- b_qkv: float32 [4224], replicated, may hold values from -3 to 3
- w_out: bfloat16 [1408, 1408], replicated, may hold values from -2.5 to 2.5
- b_out: float32 [1408], replicated, may hold values from -3 to 3
- final_gain: float32 [1408], replicated, may hold values from 0.5 to 2
- final_shift: float32 [1408], replicated, may hold values from -3 to 3
- mask_tokens: int32 [128, 192], P('clip'), parts along dimension 0, may hold values from -1 to 6143, as said below
- assignment: int32 [128], P('clip'), parts along dimension 0, may hold values from 0 to 31, each once
Outputs:
- targets: bfloat16 [128, 192, 1408], P(('clip', 'tm', 'space')), parts along dimension 0
The draws below stay inside these ranges and needn't reach their ends.
There are 4 independent parts, one for each index of `clip`. The reference program is written for one: setup_inputs(seed, part) draws one part's arguments, and reference() takes and returns one part's arrays. A program takes and returns all parts, laid end to end along the dimension named above; an argument that names none is the same for every part. Nothing has to cross between parts.
Inputs may be any that keep to these rules, and one draw needn't show every extreme that they name: `mask_tokens`: each row lists distinct tokens, no token in two rows; its listed entries come first in no fixed order, then -1 to the end. The block of tokens of one device (temporal positions k * 6 to k * 6 + 5 and patch positions m * 32 to m * 32 + 31) gives at most 6 entries to one row; in some row every such block gives exactly 6, so that row is full. `assignment`: each owner once.
All inputs are finite; a program needn't handle non-finite values.
Results may differ from the reference program's by a relative error of at most 0.0085.
The reference program's roundings to bfloat16 on the way (of `normed_in`, `projected`, `rounded`, `attended`, `hidden` and `normed`) count: a program that leaves them out, or rounds other values in their place, can miss the bound.
Values may be sent and summed in bfloat16 or wider, within the bound.
No kernel may reach another device: no remote copies, remote signals or barrier semaphores. Data moves between devices by JAX's collectives and lax.ppermute only.
A program may use at most 128 MiB of HBM per device.

```python
import math
import jax
import jax.numpy as jnp
from jax import lax

D = 1408
HEADS = 16
HD = 88
T_DEV = 6
S_DEV = 32
TEMPORAL = 24
SPATIAL = 256
TOK_DEV = 192
TOKENS = 6144
OWNERS = 32
SRC_CAP = 6
CAP = 192


def draw_activations(key, part):
    noise_key = jax.random.fold_in(key, 0)
    drawn = jnp.clip(jax.random.normal(noise_key, (TOKENS, D), jnp.float32), -6.0, 6.0)
    return drawn.reshape(TEMPORAL, SPATIAL, D).astype(jnp.bfloat16)


def draw_w_qkv(key, part):
    second_key = jax.random.fold_in(key, 1)
    third_key = jax.random.fold_in(key, 2)
    query_key_part = jnp.clip(jax.random.normal(second_key, (D, 2 * D), jnp.float32), -6.0, 6.0) * math.sqrt(1.5 / D)
    value_part = jnp.clip(jax.random.normal(third_key, (D, D), jnp.float32), -6.0, 6.0) / math.sqrt(D)
    return jnp.concatenate((query_key_part, value_part), axis=1).astype(jnp.bfloat16)


def pick_order(source_seed):
    return jax.random.permutation(source_seed, TOK_DEV)


def pick_rank(owner_seed):
    return jax.random.permutation(owner_seed, CAP)


def draw_mask_tokens(key, part):
    count_key, full_key, source_key, order_key = jax.random.split(key, 4)
    spaces = SPATIAL // S_DEV
    counts = jax.random.randint(count_key, (OWNERS, OWNERS), 0, SRC_CAP + 1)
    full_owner = jax.random.randint(full_key, (), 0, OWNERS)
    counts = jnp.where(jnp.arange(OWNERS)[:, None] == full_owner, SRC_CAP, counts)
    starts = jnp.cumsum(counts, axis=0) - counts
    orders = jax.vmap(pick_order)(jax.random.split(source_key, OWNERS))
    slots = jnp.arange(SRC_CAP)
    positions = jnp.minimum(starts[:, :, None] + slots[None, None, :], TOK_DEV - 1)
    sources = jnp.broadcast_to(jnp.arange(OWNERS)[None, :, None], positions.shape)
    local_rows = orders[sources, positions]
    frames = sources // spaces * T_DEV + local_rows // S_DEV
    patches = sources % spaces * S_DEV + local_rows % S_DEV
    token_ids = (frames * SPATIAL + patches).reshape(OWNERS, CAP)
    listed = (slots[None, None, :] < counts[:, :, None]).reshape(OWNERS, CAP)
    ranks = jax.vmap(pick_rank)(jax.random.split(order_key, OWNERS))
    sort_keys = jnp.where(listed, ranks, CAP + jnp.arange(CAP)[None, :])
    new_order = jnp.argsort(sort_keys, axis=1, stable=True)
    token_ids = jnp.take_along_axis(token_ids, new_order, axis=1)
    listed = jnp.take_along_axis(listed, new_order, axis=1)
    return jnp.where(listed, token_ids, -1).astype(jnp.int32)


def scatter_about(stream_key, dims, scale, most, dtype=jnp.bfloat16):
    result = jax.random.normal(stream_key, dims, jnp.float32) * scale
    return jnp.minimum(jnp.maximum(result, -most), most).astype(dtype)


def setup_inputs(seed: int = 0, part: int = 0) -> dict:
    splits = jax.random.split(jax.random.key(seed), 12)
    own_keys = jax.random.split(jax.random.fold_in(splits[11], part), 12)
    return {
        "activations": draw_activations(jax.random.fold_in(jax.random.fold_in(splits[11], part), 71), part),
        "attn_gain": jnp.clip(jnp.exp(jax.random.uniform(splits[1], (D,), jnp.float32, math.log(0.5), math.log(2.0))), 0.5, 2.0),
        "attn_shift": scatter_about(splits[2], (D,), 0.5, 3.0, jnp.float32),
        "w_qkv": draw_w_qkv(jax.random.fold_in(splits[11], 71), part),
        "b_qkv": scatter_about(splits[4], (3 * D,), 0.5, 3.0, jnp.float32),
        "w_out": scatter_about(splits[5], (D, D), (max(D // 256, 1)) ** -0.5, 2.5),
        "b_out": scatter_about(splits[6], (D,), 0.5, 3.0, jnp.float32),
        "final_gain": jnp.clip(jnp.exp(jax.random.uniform(splits[7], (D,), jnp.float32, math.log(0.5), math.log(2.0))), 0.5, 2.0),
        "final_shift": scatter_about(splits[8], (D,), 0.5, 3.0, jnp.float32),
        "mask_tokens": draw_mask_tokens(jax.random.fold_in(jax.random.fold_in(splits[11], part), 71), part),
        "assignment": jax.random.permutation(own_keys[10], OWNERS).astype(jnp.int32),
    }


EPSILON = 1e-06

def layer_norm(values, ln_gain, ln_shift):
    centre = lax.optimization_barrier(jnp.mean(values, axis=-1, keepdims=True))
    deviation = values - centre
    variance = lax.optimization_barrier(jnp.mean(deviation * deviation, axis=-1, keepdims=True))
    return deviation * lax.rsqrt(variance + EPSILON) * ln_gain + ln_shift

def reference(activations, attn_gain, attn_shift, w_qkv, b_qkv, w_out, b_out, final_gain, final_shift, mask_tokens, assignment):
    tokens_flat = activations.reshape(TOKENS, D)
    normed_in = layer_norm(tokens_flat.astype(jnp.float32), attn_gain, attn_shift).astype(jnp.bfloat16)
    projected = (jnp.dot(normed_in, w_qkv, preferred_element_type=jnp.float32) + b_qkv).astype(jnp.bfloat16)
    query_blocks = projected[:, :D].reshape(TOKENS // TOK_DEV, TOK_DEV, HEADS, HD)
    key_rows = projected[:, D:2 * D].reshape(TOKENS, HEADS, HD).astype(jnp.float32)
    value_rows = projected[:, 2 * D:].reshape(TOKENS, HEADS, HD).astype(jnp.float32)
    score_scale = 1.0 / math.sqrt(HD)

    def attend_block(query_block):
        scores = jnp.einsum('qhe,khe->hqk', query_block.astype(jnp.float32), key_rows) * score_scale
        highest = lax.optimization_barrier(jnp.max(scores, axis=-1, keepdims=True))
        weights = jnp.exp(scores - highest)
        totals = lax.optimization_barrier(jnp.sum(weights, axis=-1))
        rounded = lax.optimization_barrier(weights.astype(jnp.bfloat16))
        weighted = jnp.einsum('hqk,khe->hqe', rounded.astype(jnp.float32), value_rows)
        return jnp.transpose(weighted / totals[:, :, None], (1, 0, 2)).astype(jnp.bfloat16)
    attended = lax.map(attend_block, query_blocks).reshape(TOKENS, D)
    projected_out = jnp.dot(attended, w_out, preferred_element_type=jnp.float32)
    hidden = (tokens_flat.astype(jnp.float32) + projected_out + b_out).astype(jnp.bfloat16)
    normed = layer_norm(hidden.astype(jnp.float32), final_gain, final_shift).astype(jnp.bfloat16)
    owner_lists = jnp.take(mask_tokens, assignment, axis=0)
    picked = jnp.take(normed, jnp.maximum(owner_lists, 0), axis=0)
    return jnp.where((owner_lists >= 0)[:, :, None], picked, jnp.zeros_like(picked))
```

```python
import functools
import math

import jax
import jax.numpy as jnp
from jax import lax
from jax.experimental import pallas as pl
from jax.experimental.pallas import tpu as pltpu
from jax.sharding import Mesh
from jax.sharding import PartitionSpec as P

EPSILON = 1e-06
D = 1408
HEADS = 16
HD = 88
HP = 96
TOK = 192
MAIN = 128
SRC = 16
HALF = SRC * TOK
BQ = 1024
OWNERS = 32
CAP = 192
SLOTS = 24
GROUPS = 4
QK_SCALE = math.log2(math.e) / math.sqrt(HD)
SAFE = 90.0
MIB = 1 << 20

f32 = jnp.float32
bf16 = jnp.bfloat16


def params(vmem_mib):
    return pltpu.CompilerParams(vmem_limit_bytes=vmem_mib * MIB)


def vmem():
    return pl.BlockSpec(memory_space=pltpu.VMEM)


def layer_norm(values, ln_gain, ln_shift):
    centre = jnp.mean(values, axis=-1, keepdims=True)
    deviation = values - centre
    variance = jnp.mean(deviation * deviation, axis=-1, keepdims=True)
    return deviation * lax.rsqrt(variance + EPSILON) * ln_gain + ln_shift


def lanes_below(shape, bound):
    return lax.broadcasted_iota(jnp.int32, shape, 1) < bound


def column_chunks(first, count):
    done = 0
    while done < count:
        width = min(256, count - done)
        yield first + done, done, width
        done += width


def start_weights(w_ref, buffer, sems, first, count):
    copies = []
    for i, (source, target, width) in enumerate(column_chunks(first, count)):
        copy = pltpu.make_async_copy(
            w_ref.at[:, pl.ds(source, width)], buffer.at[:, pl.ds(target, width)], sems.at[i]
        )
        copy.start()
        copies.append(copy)
    return copies


def project(copies, normed, buffer, bias_ref, first, count, main, rest):
    for copy, (source, target, width) in zip(copies, column_chunks(first, count)):
        copy.wait()
        part = jnp.dot(
            normed, buffer[:, target : target + width], preferred_element_type=f32
        ) + bias_ref[:, source : source + width]
        part = part.astype(bf16).astype(f32)
        tail = part[MAIN:]
        main[target : target + width, :] = part[:MAIN].T
        rest[target : target + width, :] = jnp.concatenate((tail, tail), axis=0).T


def kv_kernel(x_ref, gain_ref, shift_ref, w_ref, bias_ref, kv_ref, normed_ref, buffer, main, rest, sems):
    copies = start_weights(w_ref, buffer, sems, D, 2 * D)
    normed = layer_norm(x_ref[...].astype(f32), gain_ref[...], shift_ref[...]).astype(bf16)
    normed_ref[...] = normed
    project(copies, normed, buffer, bias_ref, D, 2 * D, main, rest)
    ones = jnp.ones((HP - HD, 128), f32)
    low = lanes_below((HP, 128), 64)
    for h in range(HEADS):
        k_rows, v_rows = slice(h * HD, h * HD + HD), slice(D + h * HD, D + h * HD + HD)
        kv_ref[h, 0:HP, :] = jnp.concatenate((main[k_rows, :], ones), axis=0).astype(bf16)
        kv_ref[h, HP : 2 * HP, :] = jnp.concatenate((main[v_rows, :], ones), axis=0).astype(bf16)
        kv_ref[h, 2 * HP : 3 * HP, :] = jnp.where(
            low,
            jnp.concatenate((rest[k_rows, :], ones), axis=0),
            jnp.concatenate((rest[v_rows, :], ones), axis=0),
        ).astype(bf16)


def q_kernel(normed_ref, w_ref, bias_ref, q_ref, buffer, main, rest, sems):
    copies = start_weights(w_ref, buffer, sems, 0, D)
    project(copies, normed_ref[...], buffer, bias_ref, 0, D, main, rest)
    zeros = jnp.zeros((HP - HD, 128), f32)
    low = lanes_below((HP // 2, 128), 64)
    for h in range(HEADS):
        rows = slice(h * HD, h * HD + HD)
        q_ref[h, 0:HP, :] = jnp.concatenate((main[rows, :], zeros), axis=0).astype(bf16)
        tail = jnp.concatenate((rest[rows, :], zeros), axis=0)
        q_ref[h, HP : HP + HP // 2, :] = jnp.where(low, tail[: HP // 2], tail[HP // 2 :]).astype(bf16)


def unpack_pair(first, second):
    low = lanes_below(first.shape, 64)
    return (
        jnp.where(low, first, pltpu.roll(second, 64, 1)),
        jnp.where(low, pltpu.roll(first, 64, 1), second),
    )


def unpack_kv(kv_ref, keys, values):
    def put(tile, k_tile, v_tile):
        at = pl.ds(pl.multiple_of(tile * 128, 128), 128)
        turned = jnp.concatenate((k_tile, jnp.zeros((128 - HP, 128), f32)), axis=0).T.astype(bf16)
        keys[at, 0:128] = turned
        keys[at, 128:256] = turned
        values[:, at] = v_tile
        return jnp.sum(k_tile[:HD] * k_tile[:HD], axis=0, keepdims=True)

    def pair(p, largest):
        for j in (2 * p, 2 * p + 1):
            square = put(j, kv_ref[j, 0:HP, :].astype(f32), kv_ref[j, HP : 2 * HP, :])
            largest = jnp.maximum(largest, square)
        k_tile, v_tile = unpack_pair(
            kv_ref[2 * p, 2 * HP :, :].astype(f32), kv_ref[2 * p + 1, 2 * HP :, :].astype(f32)
        )
        return jnp.maximum(largest, put(SRC + p, k_tile, v_tile.astype(bf16)))

    largest = lax.fori_loop(0, SRC // 2, pair, jnp.zeros((1, 128), f32))
    return jnp.max(largest, axis=1, keepdims=True)


def unpack_q(q_ref, queries):
    def put(tile, q_tile):
        at = pl.ds(pl.multiple_of(tile * 128, 128), 128)
        scaled = q_tile * QK_SCALE
        high = scaled.astype(bf16)
        zeros = jnp.zeros((128 - HP, 128), bf16)
        queries[0:HP, at] = high
        queries[HP:128, at] = zeros
        queries[128 : 128 + HP, at] = (scaled - high.astype(f32)).astype(bf16)
        queries[128 + HP : 256, at] = zeros

    def pair(p, carried):
        put(2 * p, q_ref[2 * p, 0:HP, :].astype(f32))
        put(2 * p + 1, q_ref[2 * p + 1, 0:HP, :].astype(f32))
        top, bottom = unpack_pair(
            q_ref[2 * p, HP:, :].astype(f32), q_ref[2 * p + 1, HP:, :].astype(f32)
        )
        put(SRC + p, jnp.concatenate((top, bottom), axis=0))
        return carried

    lax.fori_loop(0, SRC // 2, pair, 0)


def set_shift(queries, at, shift):
    high = shift.astype(bf16).astype(f32)
    middle = (shift - high).astype(bf16).astype(f32)
    low = shift - high - middle
    row = lax.broadcasted_iota(jnp.int32, (8, shift.shape[1]), 0)
    rows = jnp.where(row == 0, -high, jnp.where(row == 1, -middle, jnp.where(row == 2, -low, 0.0)))
    old = queries[HP - 16 : HP, at].astype(f32)
    queries[HP - 16 : HP, at] = jnp.concatenate((old[:8], rows), axis=0).astype(bf16)


def scores_of(keys, queries, first, count, at):
    return jnp.dot(keys[pl.ds(first, count), :], queries[:, at], preferred_element_type=f32)


def keep_safe(keys, queries, at, shift_ref, acc_ref, largest_key):
    block = queries[:, at].astype(f32)
    row = lax.broadcasted_iota(jnp.int32, (128, BQ), 0)
    whole = jnp.where(row < HD, block[0:128] + block[128:256], 0.0)
    norm = jnp.sqrt(jnp.sum(whole * whole, axis=0, keepdims=True) * largest_key)
    over = jnp.max(norm * 1.01 - shift_ref[:, at])

    @pl.when(jnp.logical_not(over <= SAFE))
    def _():
        def step(i, above):
            got = scores_of(keys, queries, pl.multiple_of(i * 256, 256), 256, at)
            return jnp.maximum(above, jnp.max(got, axis=0, keepdims=True))

        above = lax.fori_loop(0, HALF // 256, step, jnp.zeros((1, BQ), f32))
        moved = shift_ref[:, at] + above
        if acc_ref is not None:
            acc_ref[:, at] = acc_ref[:, at] * jnp.exp2(-above)
        shift_ref[:, at] = moved
        set_shift(queries, at, moved)


def weighted(keys, queries, values, at):
    weights = jnp.exp2(scores_of(keys, queries, 0, HALF, at)).astype(bf16)
    return jnp.dot(values[...], weights, preferred_element_type=f32)


def own_kernel(q_ref, kv_ref, queries_ref, shift_ref, acc_ref, keys, values):
    largest_key = unpack_kv(kv_ref, keys, values)
    unpack_q(q_ref, queries_ref)

    def block(b, carried):
        at = pl.ds(pl.multiple_of(b * BQ, BQ), BQ)
        shift = jnp.max(scores_of(keys, queries_ref, 0, 256, at), axis=0, keepdims=True)
        shift_ref[:, at] = shift
        set_shift(queries_ref, at, shift)
        keep_safe(keys, queries_ref, at, shift_ref, None, largest_key)
        acc_ref[:, at] = weighted(keys, queries_ref, values, at)
        return carried

    lax.fori_loop(0, HALF // BQ, block, 0)


def other_kernel(
    kv_ref, queries_in, shift_in, acc_in, pick_ref, out_ref, keys, values, queries, shift, acc, rows
):
    largest_key = unpack_kv(kv_ref, keys, values)
    queries[...] = queries_in[...]
    shift[...] = shift_in[...]
    acc[...] = acc_in[...]

    def block(b, carried):
        at = pl.ds(pl.multiple_of(b * BQ, BQ), BQ)
        keep_safe(keys, queries, at, shift, acc, largest_key)
        total = acc[:, at] + weighted(keys, queries, values, at)
        acc[:, at] = total / total[HD : HD + 1, :]
        return carried

    lax.fori_loop(0, HALF // BQ, block, 0)
    for g in range(GROUPS):
        wanted = pick_ref[g : g + 1, :]
        picked = jnp.zeros((HP, OWNERS * SLOTS), f32)
        for first, local, count in ((512 * g, 0, 512), (2048 + 256 * g, 512, 256)):
            token = lax.broadcasted_iota(jnp.int32, (count, OWNERS * SLOTS), 0) + local
            choose = jnp.where(token == wanted, 1.0, 0.0).astype(bf16)
            picked = picked + jnp.dot(
                acc[:, first : first + count].astype(bf16), choose, preferred_element_type=f32
            )
        turned = jnp.concatenate((picked, jnp.zeros((128 - HP, OWNERS * SLOTS), f32)), axis=0).T
        rows[g] = turned

    def owner(d, carried):
        at = pl.ds(pl.multiple_of(d * SLOTS, 8), SLOTS)
        out_ref[d] = jnp.concatenate([rows[g, at, :] for g in range(GROUPS)], axis=0).astype(bf16)
        return carried

    lax.fori_loop(0, OWNERS, owner, 0)


def final_kernel(
    o_ref, act_ref, slot_ref, home_ref, w_ref, bias_ref, gain_ref, shift_ref, out_ref, attended
):
    for h in range(HEADS):
        for x in range(2):
            attended[x * 96 : x * 96 + 96, h * 128 : h * 128 + 128] = o_ref[2 * h + x]
    slot = lax.broadcasted_iota(jnp.int32, (CAP, CAP), 1)
    choose = jnp.where(slot == slot_ref[:, 0:1], 1.0, 0.0).astype(bf16)
    listed_rows = jnp.dot(choose, attended[...], preferred_element_type=f32).astype(bf16)
    place = lax.broadcasted_iota(jnp.int32, (CAP, OWNERS * 8), 1)
    choose = jnp.where(place == home_ref[:, 0:1], 1.0, 0.0).astype(bf16)
    tokens = jnp.dot(choose, act_ref[...], preferred_element_type=f32)
    hidden = tokens + jnp.dot(listed_rows, w_ref[...], preferred_element_type=f32) + bias_ref[...]
    hidden = hidden.astype(bf16).astype(f32)
    normed = layer_norm(hidden, gain_ref[...], shift_ref[...])
    out_ref[0] = jnp.where(slot_ref[:, 0:1] >= 0, normed, 0.0).astype(bf16)


def routes(mask_tokens, assignment, frames, patches, me_x, me_block):
    lists = jnp.take(mask_tokens, assignment, axis=0)
    listed = lists >= 0
    token = jnp.maximum(lists, 0)
    frame, patch = token // (patches * 8), token % (patches * 8)
    z, space = frame // frames, patch // patches
    y, x = space // 2, space % 2
    local = frame % frames * patches + patch % patches
    block = z * 8 + space
    keys = jnp.concatenate(
        (
            (z * 2 + x)[:, :, None] == jnp.arange(8)[None, None, :],
            block[:, :, None] == jnp.arange(OWNERS)[None, None, :],
        ),
        axis=-1,
    ) & listed[:, :, None]
    keys = keys.astype(bf16)
    entry = jnp.arange(CAP)
    earlier = (entry[:, None] > entry[None, :]).astype(bf16)
    before = jnp.einsum("ef,dfk->dek", earlier, keys, preferred_element_type=f32) * keys.astype(f32)
    rank = jnp.sum(before[:, :, :8], axis=-1).astype(jnp.int32)
    home_rank = jnp.sum(before[:, :, 8:], axis=-1).astype(jnp.int32)
    slot = z * SLOTS + rank
    column = jnp.where(local < MAIN, y * MAIN + local, 4 * MAIN + y * (TOK - MAIN) + local - MAIN)
    mine = listed & (x == me_x)
    hit = mine[:, :, None] & (slot[:, :, None] == jnp.arange(GROUPS * SLOTS)[None, None, :])
    pick = jnp.sum(jnp.where(hit, column[:, :, None] + 1, 0), axis=1) - 1
    pick = pick.reshape(OWNERS, GROUPS, SLOTS).transpose(1, 0, 2).reshape(GROUPS, OWNERS * SLOTS)
    here = listed & (block == me_block)
    hit = here[:, :, None] & (home_rank[:, :, None] == jnp.arange(8)[None, None, :])
    act_pick = jnp.sum(jnp.where(hit, local[:, :, None] + 1, 0), axis=1) - 1

    def own(values, base):
        row = lax.dynamic_index_in_dim(jnp.where(listed, values, base), me_block, 0, keepdims=False)
        return jnp.broadcast_to(row[:, None], (CAP, 128))

    return pick, act_pick, own(x * (GROUPS * SLOTS) + slot, -1), own(block * 8 + home_rank, -1)


def local(
    activations,
    attn_gain,
    attn_shift,
    w_qkv,
    b_qkv,
    w_out,
    b_out,
    final_gain,
    final_shift,
    mask_tokens,
    assignment,
):
    frames, patches, _ = activations.shape
    tokens = activations.reshape(TOK, D)
    heads_axes = ("tm", "y")
    all_axes = ("tm", "y", "x")
    me_x = lax.axis_index("x")
    me_block = lax.axis_index("tm") * 8 + lax.axis_index("y") * 2 + me_x

    kv_out, normed = pl.pallas_call(
        kv_kernel,
        in_specs=[vmem(), vmem(), vmem(), pl.BlockSpec(memory_space=pl.ANY), vmem()],
        out_specs=[vmem(), vmem()],
        out_shape=[
            jax.ShapeDtypeStruct((HEADS, 3 * HP, 128), bf16),
            jax.ShapeDtypeStruct((TOK, D), bf16),
        ],
        scratch_shapes=[
            pltpu.VMEM((D, 2 * D), bf16),
            pltpu.VMEM((2 * D, 128), f32),
            pltpu.VMEM((2 * D, 128), f32),
            pltpu.SemaphoreType.DMA((11,)),
        ],
        compiler_params=params(40),
        cost_estimate=pl.CostEstimate(flops=2 * TOK * D * 2 * D, bytes_accessed=9 * MIB, transcendentals=0),
        name="kv_projection",
    )(tokens, attn_gain[None], attn_shift[None], w_qkv, b_qkv[None])
    kv_in = lax.all_to_all(kv_out, heads_axes, 0, 0, tiled=True)

    q_out = pl.pallas_call(
        q_kernel,
        in_specs=[vmem(), pl.BlockSpec(memory_space=pl.ANY), vmem()],
        out_specs=vmem(),
        out_shape=jax.ShapeDtypeStruct((HEADS, HP + HP // 2, 128), bf16),
        scratch_shapes=[
            pltpu.VMEM((D, D), bf16),
            pltpu.VMEM((D, 128), f32),
            pltpu.VMEM((D, 128), f32),
            pltpu.SemaphoreType.DMA((6,)),
        ],
        compiler_params=params(24),
        cost_estimate=pl.CostEstimate(flops=2 * TOK * D * D, bytes_accessed=5 * MIB, transcendentals=0),
        name="q_projection",
    )(normed, w_qkv, b_qkv[None])
    q_out, kv_in = lax.optimization_barrier((q_out, kv_in))
    q_in = lax.all_to_all(q_out, heads_axes, 0, 0, tiled=True)
    kv_other = lax.ppermute(kv_in, "x", [(0, 1), (1, 0)])

    pick, act_pick, slot, home = routes(mask_tokens, assignment, frames, patches, me_x, me_block)
    w_padded = jnp.pad(w_out.reshape(HEADS, HD, D), ((0, 0), (0, 128 - HD), (0, 0))).reshape(HEADS * 128, D)
    act_choose = (act_pick.reshape(OWNERS * 8, 1) == jnp.arange(TOK)[None, :]).astype(bf16)
    act_out = jnp.dot(act_choose, tokens, preferred_element_type=f32).astype(bf16)
    act_out = act_out.reshape(OWNERS, 8, D)

    attend_cost = pl.CostEstimate(
        flops=4 * HALF * HALF * 256, bytes_accessed=8 * MIB, transcendentals=HALF * HALF
    )
    queries, shift, acc = pl.pallas_call(
        own_kernel,
        in_specs=[vmem(), vmem()],
        out_specs=[vmem(), vmem(), vmem()],
        out_shape=[
            jax.ShapeDtypeStruct((256, HALF), bf16),
            jax.ShapeDtypeStruct((1, HALF), f32),
            jax.ShapeDtypeStruct((HP, HALF), f32),
        ],
        scratch_shapes=[pltpu.VMEM((HALF, 256), bf16), pltpu.VMEM((HP, HALF), bf16)],
        compiler_params=params(56),
        cost_estimate=attend_cost,
        name="attend_own",
    )(q_in, kv_in)

    act_out, q_in = lax.optimization_barrier((act_out, q_in))
    act_in = lax.all_to_all(act_out, all_axes, 0, 0, tiled=True)

    o_out = pl.pallas_call(
        other_kernel,
        in_specs=[vmem()] * 5,
        out_specs=vmem(),
        out_shape=jax.ShapeDtypeStruct((OWNERS, GROUPS * SLOTS, 128), bf16),
        scratch_shapes=[
            pltpu.VMEM((HALF, 256), bf16),
            pltpu.VMEM((HP, HALF), bf16),
            pltpu.VMEM((256, HALF), bf16),
            pltpu.VMEM((1, HALF), f32),
            pltpu.VMEM((HP, HALF), f32),
            pltpu.VMEM((GROUPS, OWNERS * SLOTS, 128), f32),
        ],
        compiler_params=params(58),
        cost_estimate=attend_cost,
        name="attend_other",
    )(kv_other, queries, shift, acc, pick)
    o_in = lax.all_to_all(o_out, all_axes, 0, 0, tiled=True)

    return pl.pallas_call(
        final_kernel,
        in_specs=[vmem()] * 8,
        out_specs=vmem(),
        out_shape=jax.ShapeDtypeStruct((1, CAP, D), bf16),
        scratch_shapes=[pltpu.VMEM((CAP, HEADS * 128), bf16)],
        compiler_params=params(40),
        cost_estimate=pl.CostEstimate(flops=2 * TOK * D * D, bytes_accessed=10 * MIB, transcendentals=0),
        name="finish",
    )(
        o_in,
        act_in.reshape(OWNERS * 8, D),
        slot,
        home,
        w_padded,
        b_out[None],
        final_gain[None],
        final_shift[None],
    )


def solution(mesh):
    times, spaces, clips = (mesh.shape[a] for a in ("tm", "space", "clip"))
    fine = Mesh(mesh.devices.reshape(times, spaces // 2, 2, clips), ("tm", "y", "x", "clip"))
    in_specs = (
        P(("clip", "tm"), ("y", "x"), None),
        P(),
        P(),
        P(),
        P(),
        P(),
        P(),
        P(),
        P(),
        P("clip", None),
        P("clip"),
    )
    out_specs = P(("clip", "tm", "y", "x"), None, None)
    return jax.shard_map(local, mesh=fine, in_specs=in_specs, out_specs=out_specs, check_vma=False)
```

```python
import functools
import math

import jax
import jax.numpy as jnp
from jax import lax
from jax.experimental import pallas as pl
from jax.experimental.pallas import tpu as pltpu
from jax.sharding import Mesh
from jax.sharding import PartitionSpec as P

EPSILON = 1e-06
D = 1408
HEADS = 16
HD = 88
HP = 96
TOK = 192
MAIN = 128
OWNERS = 32
BLOCKS = 32
CAP = 192
EACH = 6
PART = 96
TOKENS = BLOCKS * TOK
COLUMNS = BLOCKS * PART
QROWS = 72
ROWS = 3 * HD + QROWS
GROUPS = 4
SLOTS = 24
WINDOW = 8 * PART + 128
BQ = 512
BK = 2048
QK_SCALE = math.log2(math.e) / math.sqrt(HD)
SAFE = 90.0
MIB = 1 << 20

f32 = jnp.float32
bf16 = jnp.bfloat16


def params(vmem_mib):
    return pltpu.CompilerParams(vmem_limit_bytes=vmem_mib * MIB)


def vmem():
    return pl.BlockSpec(memory_space=pltpu.VMEM)


def layer_norm(values, ln_gain, ln_shift):
    centre = jnp.mean(values, axis=-1, keepdims=True)
    deviation = values - centre
    variance = jnp.mean(deviation * deviation, axis=-1, keepdims=True)
    return deviation * lax.rsqrt(variance + EPSILON) * ln_gain + ln_shift


def lanes_below(shape, bound):
    return lax.broadcasted_iota(jnp.int32, shape, 1) < bound


def where_tokens(lists):
    token = jnp.maximum(lists, 0)
    frame, patch = token >> 8, token & 255
    z = (frame * 43) >> 8
    return z * 8 + (patch >> 5), (frame - z * 6) * 32 + (patch & 31)


def ones_where(condition):
    return jnp.where(condition, 1.0, 0.0)


def query_choice(lists, me):
    block, local = where_tokens(lists)
    mine = ones_where((lists >= 0) & (block == me))
    upper = ones_where(
        lax.broadcasted_iota(jnp.int32, (CAP, CAP), 0) < lax.broadcasted_iota(jnp.int32, (CAP, CAP), 1)
    )
    rank = jnp.dot(mine.astype(bf16), upper.astype(bf16), preferred_element_type=f32)
    count = jnp.sum(mine, axis=1, keepdims=True)
    lower = ones_where(
        lax.broadcasted_iota(jnp.int32, (OWNERS, OWNERS), 0)
        > lax.broadcasted_iota(jnp.int32, (OWNERS, OWNERS), 1)
    ).astype(bf16)
    bases = []
    for part in range(2):
        held = jnp.zeros_like(count)
        for k in range(part, EACH, 2):
            held = held + ones_where(count > k)
        held = jnp.broadcast_to(held, (OWNERS, 128)).astype(bf16)
        bases.append(jnp.dot(lower, held, preferred_element_type=f32)[:, 0:1] + part * PART)
    lane = lax.broadcasted_iota(jnp.int32, (OWNERS, CAP), 1).astype(f32)
    slots, tokens = [], []
    for k in range(EACH):
        token = jnp.sum(jnp.where(rank == k, mine * local.astype(f32), 0.0), axis=1, keepdims=True)
        have = count > k
        slots.append(ones_where(have & (lane == bases[k % 2] + k // 2)))
        tokens.append(ones_where(have & (lane == token)))
    return lax.dot_general(
        jnp.concatenate(slots, axis=0).astype(bf16),
        jnp.concatenate(tokens, axis=0).astype(bf16),
        (((0,), (0,)), ((), ())),
        preferred_element_type=f32,
    ).astype(bf16)


def qkv_kernel(
    me_ref, x_ref, gain_ref, shift_ref, lists_ref, w_ref, bias_ref, out_ref, buffer, main, rest, asked, sems
):
    copies = [
        pltpu.make_async_copy(w_ref.at[:, pl.ds(at, D)], buffer.at[:, pl.ds(at, D)], sems.at[i])
        for i, at in enumerate((D, 2 * D, 0))
    ]
    for copy in copies:
        copy.start()
    normed = layer_norm(x_ref[...].astype(f32), gain_ref[...][None], shift_ref[...][None]).astype(bf16)
    chosen = jnp.dot(query_choice(lists_ref[...], me_ref[0]), normed, preferred_element_type=f32)
    chosen = chosen.astype(bf16)
    for copy, at, rows in zip(copies, (D, 2 * D, 0), (normed, normed, chosen)):
        copy.wait()
        part = jnp.dot(rows, buffer[:, at : at + D], preferred_element_type=f32)
        part = (part + bias_ref[at : at + D][None]).astype(bf16).astype(f32)
        if at == 0:
            for x in range(2):
                half = part[x * PART : x * PART + PART]
                asked[x] = jnp.concatenate((half, half[:32]), axis=0).T
        else:
            tail = part[MAIN:]
            main[at - D : at, :] = part[:MAIN].T
            rest[at - D : at, :] = jnp.concatenate((tail, tail), axis=0).T
    low = lanes_below((HD, 128), 64)
    queries = lanes_below((QROWS, 128), PART)
    for h in range(HEADS):
        k_rows, v_rows = slice(h * HD, h * HD + HD), slice(D + h * HD, D + h * HD + HD)
        both = jnp.where(low, rest[k_rows, :], rest[v_rows, :])
        for x in range(2):
            top = asked[x, h * HD : h * HD + QROWS, :]
            last = jnp.concatenate(
                (asked[x, h * HD + QROWS : h * HD + HD, :], jnp.zeros((8, 128), f32)), axis=0
            )
            spread = jnp.concatenate((last, pltpu.roll(last, 64, 1), pltpu.roll(last, 32, 1)), axis=0)
            out_ref[2 * h + x] = jnp.concatenate(
                (main[k_rows, :], main[v_rows, :], both, jnp.where(queries, top, spread)), axis=0
            ).astype(bf16)


def unpack_pair(first, second):
    low = lanes_below(first.shape, 64)
    return (
        jnp.where(low, first, pltpu.roll(second, 64, 1)),
        jnp.where(low, pltpu.roll(first, 64, 1), second),
    )


def put_keys(tile, k_tile, v_tile, keys, values):
    at = pl.ds(pl.multiple_of(tile * 128, 128), 128)
    ones = jnp.ones((HP - HD, 128), f32)
    turned = jnp.concatenate((k_tile, ones, jnp.zeros((128 - HP, 128), f32)), axis=0).T.astype(bf16)
    keys[at, 0:128] = turned
    keys[at, 128:256] = turned
    values[:, at] = jnp.concatenate((v_tile, ones), axis=0).astype(bf16)
    return jnp.sum(k_tile * k_tile, axis=0, keepdims=True)


def put_queries(packed, first, count, columns):
    shape = (HD - QROWS, 128)
    parts = [
        pltpu.roll(packed[24 * i : 24 * i + HD - QROWS], 32 * (i + 1), 1) for i in range(3)
    ]
    last = jnp.where(lanes_below(shape, 32), parts[0], jnp.where(lanes_below(shape, 64), parts[1], parts[2]))
    whole = jnp.concatenate((packed, last), axis=0)
    lane = lax.broadcasted_iota(jnp.int32, whole.shape, 1)
    turn = first & 127
    turned = pltpu.roll(jnp.where(lane < count, whole, 0.0), turn, 1)
    at = pl.ds(pl.multiple_of((first >> 7) * 128, 128), 128)
    columns[:, at] = columns[:, at] + jnp.where(lane >= turn, turned, 0.0)
    at = pl.ds(pl.multiple_of((first >> 7) * 128 + 128, 128), 128)
    columns[:, at] = jnp.where(lane < turn, turned, 0.0)


def set_shift(queries, at, shift):
    high = shift.astype(bf16).astype(f32)
    middle = (shift - high).astype(bf16).astype(f32)
    low = shift - high - middle
    row = lax.broadcasted_iota(jnp.int32, (8, shift.shape[1]), 0)
    rows = jnp.where(row == 0, -high, jnp.where(row == 1, -middle, jnp.where(row == 2, -low, 0.0)))
    old = queries[HP - 16 : HP, at].astype(f32)
    queries[HP - 16 : HP, at] = jnp.concatenate((old[:8], rows), axis=0).astype(bf16)


def scores_of(keys, queries, first, count, at):
    return jnp.dot(keys[pl.ds(first, count), :], queries[:, at], preferred_element_type=f32)


def attend_columns(start, width, columns, queries, keys, values, acc, largest_key):
    at = pl.ds(pl.multiple_of(start, 256), width)
    scaled = columns[:, at] * QK_SCALE
    high = scaled.astype(bf16).astype(f32)
    zeros = jnp.zeros((128 - HD, width), f32)
    here = pl.ds(0, width)
    queries[0:128, here] = jnp.concatenate((high, zeros), axis=0).astype(bf16)
    queries[128:256, here] = jnp.concatenate((scaled - high, zeros), axis=0).astype(bf16)
    shift = jnp.max(scores_of(keys, queries, 0, 128, here), axis=0, keepdims=True)
    set_shift(queries, here, shift)
    norm = jnp.sqrt(jnp.sum(scaled * scaled, axis=0, keepdims=True) * largest_key)

    @pl.when(jnp.logical_not(jnp.max(norm * 1.01 - shift) <= SAFE))
    def _():
        def step(i, above):
            got = scores_of(keys, queries, pl.multiple_of(i * 256, 256), 256, here)
            return jnp.maximum(above, jnp.max(got, axis=0, keepdims=True))

        above = lax.fori_loop(0, TOKENS // 256, step, jnp.zeros((1, width), f32))
        set_shift(queries, here, shift + above)

    total = jnp.zeros((HP, width), f32)
    for first in range(0, TOKENS, BK):
        weights = jnp.exp2(scores_of(keys, queries, first, BK, here)).astype(bf16)
        total = total + jnp.dot(values[:, first : first + BK], weights, preferred_element_type=f32)
    acc[:, at] = total / total[HD : HD + 1, :]


def attend_kernel(first_ref, in_ref, pick_ref, out_ref, keys, values, columns, queries, acc, rows):
    columns[:, 0:128] = jnp.zeros((HD, 128), f32)

    def pair(p, largest):
        rests = []
        for j in range(2):
            block = 2 * p + j
            whole = in_ref[block].astype(f32)
            square = put_keys(block, whole[0:HD], whole[HD : 2 * HD], keys, values)
            largest = jnp.maximum(largest, square)
            rests.append(whole[2 * HD : 3 * HD])
            first = first_ref[block]
            put_queries(whole[3 * HD :], first, first_ref[block + 1] - first, columns)
        square = put_keys(BLOCKS + p, *unpack_pair(*rests), keys, values)
        return jnp.maximum(largest, square)

    largest = lax.fori_loop(0, BLOCKS // 2, pair, jnp.zeros((1, 128), f32))
    largest_key = jnp.max(largest, axis=1, keepdims=True)

    total = first_ref[BLOCKS]
    used = (total >> 7) * 128 + 128

    def clear(i, carried):
        columns[:, pl.ds(pl.multiple_of(used + i * 128, 128), 128)] = jnp.zeros((HD, 128), f32)
        return carried

    lax.fori_loop(0, 4, clear, 0)
    acc[...] = jnp.zeros_like(acc)
    blocks = (total + 255) >> 9

    def block(b, carried):
        attend_columns(b * BQ, BQ, columns, queries, keys, values, acc, largest_key)
        return carried

    lax.fori_loop(0, blocks, block, 0)

    @pl.when(total > blocks * BQ)
    def _():
        attend_columns(blocks * BQ, 256, columns, queries, keys, values, acc, largest_key)

    for g in range(GROUPS):
        begin = pl.multiple_of((first_ref[8 * g] >> 7) * 128, 128)
        near = lax.broadcasted_iota(jnp.int32, (WINDOW, OWNERS * SLOTS), 0)
        choose = ones_where(near == pick_ref[g : g + 1, :]).astype(bf16)
        picked = jnp.dot(acc[:, pl.ds(begin, WINDOW)].astype(bf16), choose, preferred_element_type=f32)
        rows[g] = jnp.concatenate((picked, jnp.zeros((128 - HP, OWNERS * SLOTS), f32)), axis=0).T

    def owner(d, carried):
        at = pl.ds(pl.multiple_of(d * SLOTS, 8), SLOTS)
        out_ref[d] = jnp.concatenate([rows[g, at, :] for g in range(GROUPS)], axis=0).astype(bf16)
        return carried

    lax.fori_loop(0, OWNERS, owner, 0)


def final_kernel(
    o_ref, act_ref, slot_ref, home_ref, w_ref, bias_ref, gain_ref, shift_ref, out_ref, attended
):
    for h in range(HEADS):
        for x in range(2):
            attended[x * 96 : x * 96 + 96, h * 128 : h * 128 + 128] = o_ref[2 * h + x]
    slot = lax.broadcasted_iota(jnp.int32, (CAP, CAP), 1)
    choose = jnp.where(slot == slot_ref[:, 0:1], 1.0, 0.0).astype(bf16)
    listed_rows = jnp.dot(choose, attended[...], preferred_element_type=f32)
    place = lax.broadcasted_iota(jnp.int32, (CAP, OWNERS * 8), 1)
    choose = jnp.where(place == home_ref[:, 0:1], 1.0, 0.0).astype(bf16)
    tokens = jnp.dot(choose, act_ref[...], preferred_element_type=f32)
    hidden = tokens + bias_ref[...][None]
    low = lanes_below((CAP, 128), HD)
    for p in range(HEADS // 2):
        first = listed_rows[:, p * 256 : p * 256 + 128]
        second = pltpu.roll(listed_rows[:, p * 256 + 128 : p * 256 + 256], HD, 1)
        both = jnp.concatenate((jnp.where(low, first, second), second), axis=1)[:, : 2 * HD]
        hidden = hidden + jnp.dot(
            both.astype(bf16), w_ref[p * 2 * HD : (p + 1) * 2 * HD, :], preferred_element_type=f32
        )
    hidden = hidden.astype(bf16).astype(f32)
    normed = layer_norm(hidden, gain_ref[...][None], shift_ref[...][None])
    out_ref[0] = jnp.where(slot_ref[:, 0:1] >= 0, normed, 0.0).astype(bf16)


def count_before(values):
    place = jnp.arange(values.shape[0])
    earlier = (place[:, None] > place[None, :]).astype(bf16)
    return jnp.dot(earlier, values.astype(bf16), preferred_element_type=f32).astype(jnp.int32)


def routes(mask_tokens, assignment, me_x, me_block):
    blocks, _ = where_tokens(mask_tokens)
    listed = mask_tokens >= 0
    hit = listed[:, :, None] & (blocks[:, :, None] == jnp.arange(BLOCKS)[None, None, :])
    count = jnp.sum(hit.astype(jnp.int32), axis=1)
    held = (count + 1 - me_x) // 2
    block_total = jnp.sum(held, axis=0)
    first = count_before(jnp.concatenate((block_total, jnp.zeros((8,), jnp.int32))))
    column = first[None, :BLOCKS] + count_before(held)
    column = column.reshape(OWNERS, GROUPS, 8) - (first[0:BLOCKS:8] // 128 * 128)[None, :, None]
    rank = jnp.arange(3)
    pick = jnp.where(
        rank < held.reshape(OWNERS, GROUPS, 8)[..., None], column[..., None] + rank, -1
    ).reshape(OWNERS, GROUPS * SLOTS)
    pick = jnp.take(pick, assignment, axis=0).reshape(OWNERS, GROUPS, SLOTS)
    pick = pick.transpose(1, 0, 2).reshape(GROUPS, OWNERS * SLOTS)

    lists = jnp.take(mask_tokens, assignment, axis=0)
    blocks, local = where_tokens(lists)
    here = (lists >= 0) & (blocks == me_block)
    entry = jnp.arange(CAP)
    earlier = (entry[:, None] < entry[None, :]).astype(bf16)
    order = jnp.dot(here.astype(bf16), earlier, preferred_element_type=f32).astype(jnp.int32)
    hit = here[:, :, None] & (order[:, :, None] == jnp.arange(8)[None, None, :])
    act_pick = jnp.sum(jnp.where(hit, local[:, :, None] + 1, 0), axis=1) - 1

    own = lax.dynamic_index_in_dim(lists, me_block, 0, keepdims=False)
    own_block, _ = where_tokens(own)
    same = (own_block[:, None] == own_block[None, :]) & (own >= 0)[:, None]
    order = jnp.sum((same & (entry[:, None] < entry[None, :])).astype(jnp.int32), axis=0)
    slot = jnp.where(own >= 0, order % 2 * PART + own_block * 3 + order // 2, -1)
    home = jnp.where(own >= 0, own_block * 8 + order, -1)
    wide = (CAP, 128)
    return (
        first,
        pick,
        act_pick,
        jnp.broadcast_to(slot[:, None], wide),
        jnp.broadcast_to(home[:, None], wide),
    )


def qkv_call(*arrays):
    return pl.pallas_call(
        qkv_kernel,
        in_specs=[pl.BlockSpec(memory_space=pltpu.SMEM)]
        + [vmem()] * 4
        + [pl.BlockSpec(memory_space=pltpu.HBM), vmem()],
        out_specs=vmem(),
        out_shape=jax.ShapeDtypeStruct((2 * HEADS, ROWS, 128), bf16),
        scratch_shapes=[
            pltpu.VMEM((D, 3 * D), bf16),
            pltpu.VMEM((2 * D, 128), f32),
            pltpu.VMEM((2 * D, 128), f32),
            pltpu.VMEM((2, D, 128), f32),
            pltpu.SemaphoreType.DMA((3,)),
        ],
        compiler_params=params(60),
        cost_estimate=pl.CostEstimate(flops=2 * TOK * D * 3 * D, bytes_accessed=14 * MIB, transcendentals=0),
        name="projection",
    )(*arrays)


def attend_call(*arrays):
    return pl.pallas_call(
        attend_kernel,
        in_specs=[pl.BlockSpec(memory_space=pltpu.SMEM), vmem(), vmem()],
        out_specs=vmem(),
        out_shape=jax.ShapeDtypeStruct((OWNERS, PART, 128), bf16),
        scratch_shapes=[
            pltpu.VMEM((TOKENS, 256), bf16),
            pltpu.VMEM((HP, TOKENS), bf16),
            pltpu.VMEM((HD, COLUMNS + 6 * 128), f32),
            pltpu.VMEM((256, BQ), bf16),
            pltpu.VMEM((HP, COLUMNS + WINDOW), f32),
            pltpu.VMEM((GROUPS, OWNERS * SLOTS, 128), f32),
        ],
        compiler_params=params(60),
        cost_estimate=pl.CostEstimate(
            flops=4 * COLUMNS * TOKENS * 256, bytes_accessed=8 * MIB, transcendentals=COLUMNS * TOKENS
        ),
        name="attend",
    )(*arrays)


def finish_call(*arrays):
    return pl.pallas_call(
        final_kernel,
        in_specs=[vmem()] * 8,
        out_specs=vmem(),
        out_shape=jax.ShapeDtypeStruct((1, CAP, D), bf16),
        scratch_shapes=[pltpu.VMEM((CAP, HEADS * 128), bf16)],
        compiler_params=params(30),
        cost_estimate=pl.CostEstimate(flops=2 * TOK * D * D, bytes_accessed=10 * MIB, transcendentals=0),
        name="finish",
    )(*arrays)


def local(
    activations,
    attn_gain,
    attn_shift,
    w_qkv,
    b_qkv,
    w_out,
    b_out,
    final_gain,
    final_shift,
    mask_tokens,
    assignment,
):
    tokens = activations.reshape(TOK, D)
    axes = ("tm", "y", "x")
    me_x = lax.axis_index("x")
    me_block = lax.axis_index("tm") * 8 + lax.axis_index("y") * 2 + me_x

    sent = qkv_call(me_block[None], tokens, attn_gain, attn_shift, mask_tokens, w_qkv, b_qkv)
    arrived = lax.all_to_all(sent, axes, 0, 0, tiled=True)

    first, pick, act_pick, slot, home = routes(mask_tokens, assignment, me_x, me_block)
    act_choose = (act_pick.reshape(OWNERS * 8, 1) == jnp.arange(TOK)[None, :]).astype(bf16)
    act_out = jnp.dot(act_choose, tokens, preferred_element_type=f32).astype(bf16)
    act_out, arrived = lax.optimization_barrier((act_out.reshape(OWNERS, 8, D), arrived))
    act_in = lax.all_to_all(act_out, axes, 0, 0, tiled=True)

    o_in = lax.all_to_all(attend_call(first, arrived, pick), axes, 0, 0, tiled=True)
    return finish_call(
        o_in, act_in.reshape(OWNERS * 8, D), slot, home, w_out, b_out, final_gain, final_shift
    )


def solution(mesh):
    times, spaces, clips = (mesh.shape[a] for a in ("tm", "space", "clip"))
    fine = Mesh(mesh.devices.reshape(times, spaces // 2, 2, clips), ("tm", "y", "x", "clip"))
    in_specs = (
        P(("clip", "tm"), ("y", "x"), None),
        P(),
        P(),
        P(),
        P(),
        P(),
        P(),
        P(),
        P(),
        P("clip", None),
        P("clip"),
    )
    out_specs = P(("clip", "tm", "y", "x"), None, None)
    return jax.shard_map(local, mesh=fine, in_specs=in_specs, out_specs=out_specs, check_vma=False)
```

```python
import functools
import math

import jax
import jax.numpy as jnp
from jax import lax
from jax.experimental import pallas as pl
from jax.experimental.pallas import tpu as pltpu
from jax.sharding import Mesh
from jax.sharding import PartitionSpec as P

EPSILON = 1e-06
D = 1408
HEADS = 16
HD = 88
HP = 96
TOK = 192
MAIN = 128
OWNERS = 32
BLOCKS = 32
CAP = 192
EACH = 6
PART = 96
TOKENS = BLOCKS * TOK
COLUMNS = BLOCKS * PART
QROWS = 72
ROWS = 3 * HD + QROWS
GROUPS = 4
PACK = 2 * QROWS
SLOTS = 24
WINDOW = 8 * PART + 128
BQ = 512
BK = 2048
QK_SCALE = math.log2(math.e) / math.sqrt(HD)
SAFE = 90.0
MIB = 1 << 20

f32 = jnp.float32
bf16 = jnp.bfloat16


def params(vmem_mib):
    return pltpu.CompilerParams(vmem_limit_bytes=vmem_mib * MIB)


def vmem():
    return pl.BlockSpec(memory_space=pltpu.VMEM)


def layer_norm(values, ln_gain, ln_shift):
    centre = jnp.mean(values, axis=-1, keepdims=True)
    deviation = values - centre
    variance = jnp.mean(deviation * deviation, axis=-1, keepdims=True)
    return deviation * lax.rsqrt(variance + EPSILON) * ln_gain + ln_shift


def lanes_below(shape, bound):
    return lax.broadcasted_iota(jnp.int32, shape, 1) < bound


def where_tokens(lists):
    token = jnp.maximum(lists, 0)
    frame, patch = token >> 8, token & 255
    z = (frame * 43) >> 8
    return z * 8 + (patch >> 5), (frame - z * 6) * 32 + (patch & 31)


def ones_where(condition):
    return jnp.where(condition, 1.0, 0.0)


def query_choice(lists, me):
    block, local = where_tokens(lists)
    mine = ones_where((lists >= 0) & (block == me))
    upper = ones_where(
        lax.broadcasted_iota(jnp.int32, (CAP, CAP), 0) < lax.broadcasted_iota(jnp.int32, (CAP, CAP), 1)
    )
    rank = jnp.dot(mine.astype(bf16), upper.astype(bf16), preferred_element_type=f32)
    count = jnp.sum(mine, axis=1, keepdims=True)
    lower = ones_where(
        lax.broadcasted_iota(jnp.int32, (OWNERS, OWNERS), 0)
        > lax.broadcasted_iota(jnp.int32, (OWNERS, OWNERS), 1)
    ).astype(bf16)
    odd = ((lax.broadcasted_iota(jnp.int32, (OWNERS, 1), 0) + me) & 1) == 1
    bases, many, few = [], jnp.zeros_like(count), jnp.zeros_like(count)
    for k in range(0, EACH, 2):
        many, few = many + ones_where(count > k), few + ones_where(count > k + 1)
    for held in (jnp.where(odd, few, many), jnp.where(odd, many, few)):
        held = jnp.broadcast_to(held, (OWNERS, 128)).astype(bf16)
        bases.append(jnp.dot(lower, held, preferred_element_type=f32)[:, 0:1] + len(bases) * PART)
    bases = (jnp.where(odd, bases[1], bases[0]), jnp.where(odd, bases[0], bases[1]))
    lane = lax.broadcasted_iota(jnp.int32, (OWNERS, CAP), 1).astype(f32)
    slots, tokens = [], []
    for k in range(EACH):
        token = jnp.sum(jnp.where(rank == k, mine * local.astype(f32), 0.0), axis=1, keepdims=True)
        have = count > k
        slots.append(ones_where(have & (lane == bases[k % 2] + k // 2)))
        tokens.append(ones_where(have & (lane == token)))
    return lax.dot_general(
        jnp.concatenate(slots, axis=0).astype(bf16),
        jnp.concatenate(tokens, axis=0).astype(bf16),
        (((0,), (0,)), ((), ())),
        preferred_element_type=f32,
    ).astype(bf16)


def qkv_kernel(
    me_ref, x_ref, gain_ref, shift_ref, lists_ref, w_ref, bias_ref, out_ref, buffer, main, rest, asked, sems
):
    copies = [
        pltpu.make_async_copy(w_ref.at[:, pl.ds(at, D)], buffer.at[:, pl.ds(at, D)], sems.at[i])
        for i, at in enumerate((D, 2 * D, 0))
    ]
    for copy in copies:
        copy.start()
    normed = layer_norm(x_ref[...].astype(f32), gain_ref[...][None], shift_ref[...][None]).astype(bf16)
    chosen = jnp.dot(query_choice(lists_ref[...], me_ref[0]), normed, preferred_element_type=f32)
    chosen = chosen.astype(bf16)
    for copy, at, rows in zip(copies, (D, 2 * D, 0), (normed, normed, chosen)):
        copy.wait()
        part = jnp.dot(rows, buffer[:, at : at + D], preferred_element_type=f32)
        part = (part + bias_ref[at : at + D][None]).astype(bf16).astype(f32)
        if at == 0:
            for x in range(2):
                half = part[x * PART : x * PART + PART]
                asked[x] = jnp.concatenate((half, half[:32]), axis=0).T
        else:
            tail = part[MAIN:]
            main[at - D : at, :] = part[:MAIN].T
            rest[at - D : at, :] = jnp.concatenate((tail, tail), axis=0).T
    low = lanes_below((HD, 128), 64)
    queries = lanes_below((QROWS, 128), PART)
    for h in range(HEADS):
        k_rows, v_rows = slice(h * HD, h * HD + HD), slice(D + h * HD, D + h * HD + HD)
        both = jnp.where(low, rest[k_rows, :], rest[v_rows, :])
        for x in range(2):
            top = asked[x, h * HD : h * HD + QROWS, :]
            last = jnp.concatenate(
                (asked[x, h * HD + QROWS : h * HD + HD, :], jnp.zeros((8, 128), f32)), axis=0
            )
            spread = jnp.concatenate((last, pltpu.roll(last, 64, 1), pltpu.roll(last, 32, 1)), axis=0)
            out_ref[2 * h + x] = jnp.concatenate(
                (main[k_rows, :], main[v_rows, :], both, jnp.where(queries, top, spread)), axis=0
            ).astype(bf16)


def unpack_pair(first, second):
    low = lanes_below(first.shape, 64)
    return (
        jnp.where(low, first, pltpu.roll(second, 64, 1)),
        jnp.where(low, pltpu.roll(first, 64, 1), second),
    )


def put_keys(tile, k_tile, v_tile, keys, values):
    at = pl.ds(pl.multiple_of(tile * 128, 128), 128)
    ones = jnp.ones((HP - HD, 128), f32)
    turned = jnp.concatenate((k_tile, ones, jnp.zeros((128 - HP, 128), f32)), axis=0).T.astype(bf16)
    keys[at, 0:128] = turned
    keys[at, 128:256] = turned
    values[:, at] = jnp.concatenate((v_tile, ones), axis=0).astype(bf16)
    return jnp.sum(k_tile * k_tile, axis=0, keepdims=True)


def put_queries(packed, first, count, columns):
    shape = (HD - QROWS, 128)
    parts = [
        pltpu.roll(packed[24 * i : 24 * i + HD - QROWS], 32 * (i + 1), 1) for i in range(3)
    ]
    last = jnp.where(lanes_below(shape, 32), parts[0], jnp.where(lanes_below(shape, 64), parts[1], parts[2]))
    whole = jnp.concatenate((packed, last), axis=0)
    lane = lax.broadcasted_iota(jnp.int32, whole.shape, 1)
    turn = first & 127
    turned = pltpu.roll(jnp.where(lane < count, whole, 0.0), turn, 1)
    at = pl.ds(pl.multiple_of((first >> 7) * 128, 128), 128)
    columns[:, at] = columns[:, at] + jnp.where(lane >= turn, turned, 0.0)
    at = pl.ds(pl.multiple_of((first >> 7) * 128 + 128, 128), 128)
    columns[:, at] = jnp.where(lane < turn, turned, 0.0)


def set_shift(queries, at, shift):
    high = shift.astype(bf16).astype(f32)
    middle = (shift - high).astype(bf16).astype(f32)
    low = shift - high - middle
    row = lax.broadcasted_iota(jnp.int32, (8, shift.shape[1]), 0)
    rows = jnp.where(row == 0, -high, jnp.where(row == 1, -middle, jnp.where(row == 2, -low, 0.0)))
    old = queries[HP - 16 : HP, at].astype(f32)
    queries[HP - 16 : HP, at] = jnp.concatenate((old[:8], rows), axis=0).astype(bf16)


def scores_of(keys, queries, first, count, at):
    return jnp.dot(keys[pl.ds(first, count), :], queries[:, at], preferred_element_type=f32)


def attend_columns(start, width, columns, queries, keys, values, acc, largest_key):
    at = pl.ds(pl.multiple_of(start, 256), width)
    scaled = columns[:, at] * QK_SCALE
    high = scaled.astype(bf16).astype(f32)
    zeros = jnp.zeros((128 - HD, width), f32)
    here = pl.ds(0, width)
    queries[0:128, here] = jnp.concatenate((high, zeros), axis=0).astype(bf16)
    queries[128:256, here] = jnp.concatenate((scaled - high, zeros), axis=0).astype(bf16)
    shift = jnp.max(scores_of(keys, queries, 0, 128, here), axis=0, keepdims=True)
    set_shift(queries, here, shift)
    norm = jnp.sqrt(jnp.sum(scaled * scaled, axis=0, keepdims=True) * largest_key)

    @pl.when(jnp.logical_not(jnp.max(norm * 1.01 - shift) <= SAFE))
    def _():
        def step(i, above):
            got = scores_of(keys, queries, pl.multiple_of(i * 256, 256), 256, here)
            return jnp.maximum(above, jnp.max(got, axis=0, keepdims=True))

        above = lax.fori_loop(0, TOKENS // 256, step, jnp.zeros((1, width), f32))
        set_shift(queries, here, shift + above)

    total = jnp.zeros((HP, width), f32)
    for first in range(0, TOKENS, BK):
        weights = jnp.exp2(scores_of(keys, queries, first, BK, here)).astype(bf16)
        total = total + jnp.dot(values[:, first : first + BK], weights, preferred_element_type=f32)
    acc[:, at] = total / total[HD : HD + 1, :]


def attend_kernel(first_ref, in_ref, pick_ref, act_ref, out_ref, keys, values, columns, queries, acc, rows):
    columns[:, 0:128] = jnp.zeros((HD, 128), f32)

    def pair(p, largest):
        rests = []
        for j in range(2):
            block = 2 * p + j
            whole = in_ref[block].astype(f32)
            square = put_keys(block, whole[0:HD], whole[HD : 2 * HD], keys, values)
            largest = jnp.maximum(largest, square)
            rests.append(whole[2 * HD : 3 * HD])
            first = first_ref[block]
            put_queries(whole[3 * HD :], first, first_ref[block + 1] - first, columns)
        square = put_keys(BLOCKS + p, *unpack_pair(*rests), keys, values)
        return jnp.maximum(largest, square)

    largest = lax.fori_loop(0, BLOCKS // 2, pair, jnp.zeros((1, 128), f32))
    largest_key = jnp.max(largest, axis=1, keepdims=True)

    total = first_ref[BLOCKS]
    used = (total >> 7) * 128 + 128

    def clear(i, carried):
        columns[:, pl.ds(pl.multiple_of(used + i * 128, 128), 128)] = jnp.zeros((HD, 128), f32)
        return carried

    lax.fori_loop(0, 4, clear, 0)
    acc[...] = jnp.zeros_like(acc)
    blocks = (total + 255) >> 9

    def block(b, carried):
        attend_columns(b * BQ, BQ, columns, queries, keys, values, acc, largest_key)
        return carried

    lax.fori_loop(0, blocks, block, 0)

    @pl.when(total > blocks * BQ)
    def _():
        attend_columns(blocks * BQ, 256, columns, queries, keys, values, acc, largest_key)

    for g in range(GROUPS):
        begin = pl.multiple_of((first_ref[8 * g] >> 7) * 128, 128)
        near = lax.broadcasted_iota(jnp.int32, (WINDOW, OWNERS * SLOTS), 0)
        choose = ones_where(near == pick_ref[g : g + 1, :]).astype(bf16)
        picked = jnp.dot(acc[:, pl.ds(begin, WINDOW)].astype(bf16), choose, preferred_element_type=f32)
        rows[g] = jnp.concatenate((picked, jnp.zeros((128 - HP, OWNERS * SLOTS), f32)), axis=0).T

    def owner(d, carried):
        at = pl.ds(pl.multiple_of(d * SLOTS, 8), SLOTS)
        found = jnp.concatenate([rows[g, at, :] for g in range(GROUPS - 1)], axis=0)
        last = rows[GROUPS - 1, at, :]
        spread = jnp.concatenate([pltpu.roll(last, HD - 40 * i, 1) for i in range(3)], axis=0)
        packed = jnp.where(lanes_below((QROWS, 128), HD), found, spread)
        out_ref[d] = jnp.concatenate((packed, act_ref[d].astype(f32)), axis=0).astype(bf16)
        return carried

    lax.fori_loop(0, OWNERS, owner, 0)


def final_kernel(
    in_ref, slot_ref, home_ref, w_ref, bias_ref, gain_ref, shift_ref, out_ref, attended, acts
):
    shape = (SLOTS, 128)
    for h in range(HEADS):
        for x in range(2):
            whole = in_ref[2 * h + x].astype(f32)
            parts = [pltpu.roll(whole[SLOTS * i : SLOTS * i + SLOTS], 40 * (i + 1), 1) for i in range(3)]
            last = jnp.where(
                lanes_below(shape, 40), parts[0], jnp.where(lanes_below(shape, 80), parts[1], parts[2])
            )
            attended[x * PART : x * PART + PART, h * 128 : h * 128 + 128] = jnp.concatenate(
                (whole[:QROWS], last), axis=0
            ).astype(bf16)
            at = 8 * (2 * h + x)
            for c in range(9):
                acts[at : at + 8, c * 128 : c * 128 + 128] = whole[QROWS + 8 * c : QROWS + 8 * c + 8]
    slot = lax.broadcasted_iota(jnp.int32, (CAP, CAP), 1)
    choose = ones_where(slot == slot_ref[:, 0:1]).astype(bf16)
    listed_rows = jnp.dot(choose, attended[...], preferred_element_type=f32)
    place = lax.broadcasted_iota(jnp.int32, (CAP, BLOCKS * 8), 1)
    home = home_ref[:, 0:1]
    choose = ones_where(place == home).astype(bf16)
    got = acts[...].astype(bf16)
    tokens = jnp.dot(choose, got, preferred_element_type=f32)
    tail = jnp.zeros((CAP, 256), f32)
    rank = home & 7
    for i in range(3):
        there = jnp.where((home >= 0) & (rank >> 1 == i), home - rank + EACH + (rank & 1), -1)
        choose = ones_where(place == there).astype(bf16)
        pair = jnp.concatenate(
            (got[:, i * 128 : i * 128 + 128], got[:, (i + 3) * 128 : (i + 4) * 128]), axis=1
        )
        tail = tail + jnp.dot(choose, pair, preferred_element_type=f32)
    tokens = jnp.concatenate((tokens, tail), axis=1)
    hidden = tokens + bias_ref[...][None]
    low = lanes_below((CAP, 128), HD)
    for p in range(HEADS // 2):
        first = listed_rows[:, p * 256 : p * 256 + 128]
        second = pltpu.roll(listed_rows[:, p * 256 + 128 : p * 256 + 256], HD, 1)
        both = jnp.concatenate((jnp.where(low, first, second), second), axis=1)[:, : 2 * HD]
        hidden = hidden + jnp.dot(
            both.astype(bf16), w_ref[p * 2 * HD : (p + 1) * 2 * HD, :], preferred_element_type=f32
        )
    hidden = hidden.astype(bf16).astype(f32)
    normed = layer_norm(hidden, gain_ref[...][None], shift_ref[...][None])
    out_ref[0] = jnp.where(slot_ref[:, 0:1] >= 0, normed, 0.0).astype(bf16)


def count_before(values):
    place = jnp.arange(values.shape[0])
    earlier = (place[:, None] > place[None, :]).astype(bf16)
    return jnp.dot(earlier, values.astype(bf16), preferred_element_type=f32).astype(jnp.int32)


def routes(mask_tokens, assignment, me_x, me_block):
    blocks, _ = where_tokens(mask_tokens)
    listed = mask_tokens >= 0
    hit = listed[:, :, None] & (blocks[:, :, None] == jnp.arange(BLOCKS)[None, None, :])
    count = jnp.sum(hit.astype(jnp.int32), axis=1)
    odd = (jnp.arange(OWNERS)[:, None] + jnp.arange(BLOCKS)[None, :]) % 2
    held = (count + (odd == me_x)) // 2
    block_total = jnp.sum(held, axis=0)
    first = count_before(jnp.concatenate((block_total, jnp.zeros((8,), jnp.int32))))
    column = first[None, :BLOCKS] + count_before(held)
    column = column.reshape(OWNERS, GROUPS, 8) - (first[0:BLOCKS:8] // 128 * 128)[None, :, None]
    rank = jnp.arange(3)
    pick = jnp.where(
        rank < held.reshape(OWNERS, GROUPS, 8)[..., None], column[..., None] + rank, -1
    ).reshape(OWNERS, GROUPS * SLOTS)
    pick = jnp.take(pick, assignment, axis=0).reshape(OWNERS, GROUPS, SLOTS)
    pick = pick.transpose(1, 0, 2).reshape(GROUPS, OWNERS * SLOTS)

    lists = jnp.take(mask_tokens, assignment, axis=0)
    blocks, local = where_tokens(lists)
    here = (lists >= 0) & (blocks == me_block)
    entry = jnp.arange(CAP)
    earlier = (entry[:, None] < entry[None, :]).astype(bf16)
    order = jnp.dot(here.astype(bf16), earlier, preferred_element_type=f32).astype(jnp.int32)
    hit = here[:, :, None] & (order[:, :, None] == jnp.arange(8)[None, None, :])
    act_pick = jnp.sum(jnp.where(hit, local[:, :, None] + 1, 0), axis=1) - 1

    own = lax.dynamic_index_in_dim(lists, me_block, 0, keepdims=False)
    own_block, _ = where_tokens(own)
    same = (own_block[:, None] == own_block[None, :]) & (own >= 0)[:, None]
    order = jnp.sum((same & (entry[:, None] < entry[None, :])).astype(jnp.int32), axis=0)
    half = (order + own_block + lax.dynamic_index_in_dim(assignment, me_block, 0, keepdims=False)) % 2
    slot = jnp.where(own >= 0, half * PART + own_block * 3 + order // 2, -1)
    home = jnp.where(own >= 0, own_block * 8 + order, -1)
    wide = (CAP, 128)
    return (
        first,
        pick,
        act_pick,
        jnp.broadcast_to(slot[:, None], wide),
        jnp.broadcast_to(home[:, None], wide),
    )


def pack_rows(act_pick, tokens):
    choose = (act_pick[:, :EACH].reshape(OWNERS * EACH, 1) == jnp.arange(TOK)[None, :]).astype(bf16)
    found = jnp.dot(choose, tokens, preferred_element_type=f32).astype(bf16)
    tiles = found.reshape(OWNERS, EACH, 11, 128).transpose(0, 2, 1, 3)
    last = tiles[:, 9:].reshape(OWNERS, EACH, 2, 128)
    last = jnp.concatenate((last, jnp.zeros((OWNERS, 3, 2, 128), bf16)), axis=1)
    return jnp.concatenate((tiles[:, :9], last), axis=2).reshape(OWNERS, QROWS, 128)


def qkv_call(*arrays):
    return pl.pallas_call(
        qkv_kernel,
        in_specs=[pl.BlockSpec(memory_space=pltpu.SMEM)]
        + [vmem()] * 4
        + [pl.BlockSpec(memory_space=pltpu.HBM), vmem()],
        out_specs=vmem(),
        out_shape=jax.ShapeDtypeStruct((2 * HEADS, ROWS, 128), bf16),
        scratch_shapes=[
            pltpu.VMEM((D, 3 * D), bf16),
            pltpu.VMEM((2 * D, 128), f32),
            pltpu.VMEM((2 * D, 128), f32),
            pltpu.VMEM((2, D, 128), f32),
            pltpu.SemaphoreType.DMA((3,)),
        ],
        compiler_params=params(60),
        cost_estimate=pl.CostEstimate(flops=2 * TOK * D * 3 * D, bytes_accessed=14 * MIB, transcendentals=0),
        name="projection",
    )(*arrays)


def attend_call(*arrays):
    return pl.pallas_call(
        attend_kernel,
        in_specs=[pl.BlockSpec(memory_space=pltpu.SMEM), vmem(), vmem(), vmem()],
        out_specs=vmem(),
        out_shape=jax.ShapeDtypeStruct((OWNERS, PACK, 128), bf16),
        scratch_shapes=[
            pltpu.VMEM((TOKENS, 256), bf16),
            pltpu.VMEM((HP, TOKENS), bf16),
            pltpu.VMEM((HD, COLUMNS + 6 * 128), f32),
            pltpu.VMEM((256, BQ), bf16),
            pltpu.VMEM((HP, COLUMNS + WINDOW), f32),
            pltpu.VMEM((GROUPS, OWNERS * SLOTS, 128), f32),
        ],
        compiler_params=params(30),
        cost_estimate=pl.CostEstimate(
            flops=4 * COLUMNS * TOKENS * 256, bytes_accessed=8 * MIB, transcendentals=COLUMNS * TOKENS
        ),
        name="attend",
    )(*arrays)


def finish_call(*arrays):
    return pl.pallas_call(
        final_kernel,
        in_specs=[vmem()] * 7,
        out_specs=vmem(),
        out_shape=jax.ShapeDtypeStruct((1, CAP, D), bf16),
        scratch_shapes=[pltpu.VMEM((CAP, HEADS * 128), bf16), pltpu.VMEM((BLOCKS * 8, 9 * 128), f32)],
        compiler_params=params(30),
        cost_estimate=pl.CostEstimate(flops=2 * TOK * D * D, bytes_accessed=10 * MIB, transcendentals=0),
        name="finish",
    )(*arrays)


def local(
    activations,
    attn_gain,
    attn_shift,
    w_qkv,
    b_qkv,
    w_out,
    b_out,
    final_gain,
    final_shift,
    mask_tokens,
    assignment,
):
    tokens = activations.reshape(TOK, D)
    axes = ("tm", "y", "x")
    me_x = lax.axis_index("x")
    me_block = lax.axis_index("tm") * 8 + lax.axis_index("y") * 2 + me_x

    sent = qkv_call(me_block[None], tokens, attn_gain, attn_shift, mask_tokens, w_qkv, b_qkv)
    arrived = lax.all_to_all(sent, axes, 0, 0, tiled=True)

    first, pick, act_pick, slot, home = routes(mask_tokens, assignment, me_x, me_block)
    act_out = pack_rows(act_pick, tokens)
    first, pick, act_out, slot, home = lax.optimization_barrier((first, pick, act_out, slot, home))
    o_in = lax.all_to_all(attend_call(first, arrived, pick, act_out), axes, 0, 0, tiled=True)
    return finish_call(o_in, slot, home, w_out, b_out, final_gain, final_shift)


def solution(mesh):
    times, spaces, clips = (mesh.shape[a] for a in ("tm", "space", "clip"))
    fine = Mesh(mesh.devices.reshape(times, spaces // 2, 2, clips), ("tm", "y", "x", "clip"))
    in_specs = (
        P(("clip", "tm"), ("y", "x"), None),
        P(),
        P(),
        P(),
        P(),
        P(),
        P(),
        P(),
        P(),
        P("clip", None),
        P("clip"),
    )
    out_specs = P(("clip", "tm", "y", "x"), None, None)
    return jax.shard_map(local, mesh=fine, in_specs=in_specs, out_specs=out_specs, check_vma=False)
```

```python
import functools
import math

import jax
import jax.numpy as jnp
from jax import lax
from jax.experimental import pallas as pl
from jax.experimental.pallas import tpu as pltpu
from jax.sharding import Mesh
from jax.sharding import PartitionSpec as P

EPSILON = 1e-06
D = 1408
HEADS = 16
HD = 88
HP = 96
TOK = 192
MAIN = 128
OWNERS = 32
BLOCKS = 32
CAP = 192
EACH = 6
PART = 96
TOKENS = BLOCKS * TOK
COLUMNS = BLOCKS * PART
QROWS = 72
ROWS = 3 * HD + QROWS
GROUPS = 4
PACK = 2 * QROWS
SLOTS = 24
WINDOW = 8 * PART + 128
BQ = 512
BK = 2048
QK_SCALE = math.log2(math.e) / math.sqrt(HD)
SAFE = 90.0
MIB = 1 << 20

f32 = jnp.float32
bf16 = jnp.bfloat16


def params(vmem_mib):
    return pltpu.CompilerParams(vmem_limit_bytes=vmem_mib * MIB)


def vmem():
    return pl.BlockSpec(memory_space=pltpu.VMEM)


def layer_norm(values, ln_gain, ln_shift):
    centre = jnp.mean(values, axis=-1, keepdims=True)
    deviation = values - centre
    variance = jnp.mean(deviation * deviation, axis=-1, keepdims=True)
    return deviation * lax.rsqrt(variance + EPSILON) * ln_gain + ln_shift


def lanes_below(shape, bound):
    return lax.broadcasted_iota(jnp.int32, shape, 1) < bound


def where_tokens(lists):
    token = jnp.maximum(lists, 0)
    frame, patch = token >> 8, token & 255
    z = (frame * 43) >> 8
    return z * 8 + (patch >> 5), (frame - z * 6) * 32 + (patch & 31)


def ones_where(condition):
    return jnp.where(condition, 1.0, 0.0)


def query_choice(lists, me):
    block, local = where_tokens(lists)
    mine = ones_where((lists >= 0) & (block == me))
    upper = ones_where(
        lax.broadcasted_iota(jnp.int32, (CAP, CAP), 0) < lax.broadcasted_iota(jnp.int32, (CAP, CAP), 1)
    )
    rank = jnp.dot(mine.astype(bf16), upper.astype(bf16), preferred_element_type=f32)
    count = jnp.sum(mine, axis=1, keepdims=True)
    lower = ones_where(
        lax.broadcasted_iota(jnp.int32, (OWNERS, OWNERS), 0)
        > lax.broadcasted_iota(jnp.int32, (OWNERS, OWNERS), 1)
    ).astype(bf16)
    odd = ((lax.broadcasted_iota(jnp.int32, (OWNERS, 1), 0) + me) & 1) == 1
    bases, many, few = [], jnp.zeros_like(count), jnp.zeros_like(count)
    for k in range(0, EACH, 2):
        many, few = many + ones_where(count > k), few + ones_where(count > k + 1)
    for held in (jnp.where(odd, few, many), jnp.where(odd, many, few)):
        held = jnp.broadcast_to(held, (OWNERS, 128)).astype(bf16)
        bases.append(jnp.dot(lower, held, preferred_element_type=f32)[:, 0:1] + len(bases) * PART)
    bases = (jnp.where(odd, bases[1], bases[0]), jnp.where(odd, bases[0], bases[1]))
    lane = lax.broadcasted_iota(jnp.int32, (OWNERS, CAP), 1).astype(f32)
    slots, tokens = [], []
    for k in range(EACH):
        token = jnp.sum(jnp.where(rank == k, mine * local.astype(f32), 0.0), axis=1, keepdims=True)
        have = count > k
        slots.append(ones_where(have & (lane == bases[k % 2] + k // 2)))
        tokens.append(ones_where(have & (lane == token)))
    return lax.dot_general(
        jnp.concatenate(slots, axis=0).astype(bf16),
        jnp.concatenate(tokens, axis=0).astype(bf16),
        (((0,), (0,)), ((), ())),
        preferred_element_type=f32,
    ).astype(bf16)


def qkv_kernel(
    me_ref, x_ref, gain_ref, shift_ref, lists_ref, w_ref, bias_ref, out_ref, buffer, main, rest, asked, sems
):
    copies = [
        pltpu.make_async_copy(w_ref.at[:, pl.ds(at, D)], buffer.at[:, pl.ds(at, D)], sems.at[i])
        for i, at in enumerate((D, 2 * D, 0))
    ]
    for copy in copies:
        copy.start()
    normed = layer_norm(x_ref[...].astype(f32), gain_ref[...][None], shift_ref[...][None]).astype(bf16)
    chosen = jnp.dot(query_choice(lists_ref[...], me_ref[0]), normed, preferred_element_type=f32)
    chosen = chosen.astype(bf16)
    for copy, at, rows in zip(copies, (D, 2 * D, 0), (normed, normed, chosen)):
        copy.wait()
        part = jnp.dot(rows, buffer[:, at : at + D], preferred_element_type=f32)
        part = (part + bias_ref[at : at + D][None]).astype(bf16).astype(f32)
        if at == 0:
            for x in range(2):
                half = part[x * PART : x * PART + PART]
                asked[x] = jnp.concatenate((half, half[:32]), axis=0).T
        else:
            tail = part[MAIN:]
            main[at - D : at, :] = part[:MAIN].T
            rest[at - D : at, :] = jnp.concatenate((tail, tail), axis=0).T
    low = lanes_below((HD, 128), 64)
    queries = lanes_below((QROWS, 128), PART)
    for h in range(HEADS):
        k_rows, v_rows = slice(h * HD, h * HD + HD), slice(D + h * HD, D + h * HD + HD)
        both = jnp.where(low, rest[k_rows, :], rest[v_rows, :])
        for x in range(2):
            top = asked[x, h * HD : h * HD + QROWS, :]
            last = jnp.concatenate(
                (asked[x, h * HD + QROWS : h * HD + HD, :], jnp.zeros((8, 128), f32)), axis=0
            )
            spread = jnp.concatenate((last, pltpu.roll(last, 64, 1), pltpu.roll(last, 32, 1)), axis=0)
            out_ref[2 * h + x] = jnp.concatenate(
                (main[k_rows, :], main[v_rows, :], both, jnp.where(queries, top, spread)), axis=0
            ).astype(bf16)


def unpack_pair(first, second):
    low = lanes_below(first.shape, 64)
    return (
        jnp.where(low, first, pltpu.roll(second, 64, 1)),
        jnp.where(low, pltpu.roll(first, 64, 1), second),
    )


def put_keys(tile, k_tile, v_tile, keys, values):
    at = pl.ds(tile * 128, 128)
    ones = jnp.ones((HP - HD, 128), f32)
    turned = jnp.concatenate((k_tile, ones, jnp.zeros((128 - HP, 128), f32)), axis=0).T.astype(bf16)
    keys[at, 0:128] = turned
    keys[at, 128:256] = turned
    values[:, at] = jnp.concatenate((v_tile, ones), axis=0).astype(bf16)
    return jnp.sum(k_tile * k_tile, axis=0, keepdims=True)


def put_queries(packed, first, count, columns):
    shape = (HD - QROWS, 128)
    parts = [
        pltpu.roll(packed[24 * i : 24 * i + HD - QROWS], 32 * (i + 1), 1) for i in range(3)
    ]
    last = jnp.where(lanes_below(shape, 32), parts[0], jnp.where(lanes_below(shape, 64), parts[1], parts[2]))
    whole = jnp.concatenate((packed, last), axis=0)
    lane = lax.broadcasted_iota(jnp.int32, whole.shape, 1)
    turn = first & 127
    turned = pltpu.roll(jnp.where(lane < count, whole, 0.0), turn, 1)
    at = pl.ds(pl.multiple_of((first >> 7) * 128, 128), 128)
    columns[:, at] = columns[:, at] + jnp.where(lane >= turn, turned, 0.0)
    at = pl.ds(pl.multiple_of((first >> 7) * 128 + 128, 128), 128)
    columns[:, at] = jnp.where(lane < turn, turned, 0.0)


def set_shift(queries, at, shift):
    high = shift.astype(bf16).astype(f32)
    middle = (shift - high).astype(bf16).astype(f32)
    low = shift - high - middle
    row = lax.broadcasted_iota(jnp.int32, (8, shift.shape[1]), 0)
    rows = jnp.where(row == 0, -high, jnp.where(row == 1, -middle, jnp.where(row == 2, -low, 0.0)))
    old = queries[HP - 16 : HP, at].astype(f32)
    queries[HP - 16 : HP, at] = jnp.concatenate((old[:8], rows), axis=0).astype(bf16)


def scores_of(keys, queries, first, count, at):
    return jnp.dot(keys[pl.ds(first, count), :], queries[:, at], preferred_element_type=f32)


def start_columns(at, columns, queries, keys):
    scaled = columns[:, at] * QK_SCALE
    high = scaled.astype(bf16).astype(f32)
    width = scaled.shape[1]
    zeros = jnp.zeros((128 - HD, width), f32)
    here = pl.ds(0, width)
    queries[0:128, here] = jnp.concatenate((high, zeros), axis=0).astype(bf16)
    queries[128:256, here] = jnp.concatenate((scaled - high, zeros), axis=0).astype(bf16)
    shift = jnp.max(scores_of(keys, queries, 0, 128, here), axis=0, keepdims=True)
    set_shift(queries, here, shift)
    return shift, jnp.sum(scaled * scaled, axis=0, keepdims=True)


def unsafe(shift, square, largest_key):
    return jnp.logical_not(jnp.max(jnp.sqrt(square * largest_key) * 1.01 - shift) <= SAFE)


def weigh(keys, queries, values, first, width):
    weights = jnp.exp2(scores_of(keys, queries, first, BK, pl.ds(0, width))).astype(bf16)
    return jnp.dot(values[:, first : first + BK], weights, preferred_element_type=f32)


def attend_columns(start, width, columns, queries, keys, values, acc, largest_key):
    at = pl.ds(pl.multiple_of(start, 256), width)
    here = pl.ds(0, width)
    shift, square = start_columns(at, columns, queries, keys)

    @pl.when(unsafe(shift, square, largest_key))
    def _():
        def step(i, above):
            got = scores_of(keys, queries, pl.multiple_of(i * 256, 256), 256, here)
            return jnp.maximum(above, jnp.max(got, axis=0, keepdims=True))

        above = lax.fori_loop(0, TOKENS // 256, step, jnp.zeros((1, width), f32))
        set_shift(queries, here, shift + above)

    total = weigh(keys, queries, values, 0, width)
    for first in range(BK, TOKENS, BK):
        total = total + weigh(keys, queries, values, first, width)
    acc[:, at] = total / total[HD : HD + 1, :]


def unpack_keys(chunk, in_ref, keys, values):
    largest = jnp.zeros((1, 128), f32)
    for i in range(BLOCKS // 2):
        if chunk < 2:
            block = chunk * (BLOCKS // 2) + i
            k_tile = in_ref[block, 0:96].astype(f32)[:HD]
            v_tile = in_ref[block, 80:176].astype(f32)[8:]
        else:
            rests = [in_ref[2 * i + j, 176:272].astype(f32)[:HD] for j in range(2)]
            k_tile, v_tile = unpack_pair(*rests)
        square = put_keys(chunk * (BLOCKS // 2) + i, k_tile, v_tile, keys, values)
        largest = jnp.maximum(largest, square)
    return largest


def attend_kernel(
    first_ref, in_ref, pick_ref, act_ref, out_ref, keys, values, columns, queries, acc, rows
):
    columns[:, 0:128] = jnp.zeros((HD, 128), f32)

    def place(block, carried):
        first = first_ref[block]
        packed = in_ref[block, 256:336].astype(f32)[8:]
        put_queries(packed, first, first_ref[block + 1] - first, columns)
        return carried

    lax.fori_loop(0, BLOCKS, place, 0, unroll=8)
    total = first_ref[BLOCKS]
    used = (total >> 7) * 128 + 128

    def clear(i, carried):
        columns[:, pl.ds(pl.multiple_of(used + i * 128, 128), 128)] = jnp.zeros((HD, 128), f32)
        return carried

    lax.fori_loop(0, 4, clear, 0)
    acc[...] = jnp.zeros_like(acc)

    largest = unpack_keys(0, in_ref, keys, values)
    shift, square = start_columns(pl.ds(0, BQ), columns, queries, keys)
    found = weigh(keys, queries, values, 0, BQ)
    for chunk in (1, 2):
        largest = jnp.maximum(largest, unpack_keys(chunk, in_ref, keys, values))
        found = found + weigh(keys, queries, values, chunk * BK, BQ)
    acc[:, 0:BQ] = found / found[HD : HD + 1, :]
    largest_key = jnp.max(largest, axis=1, keepdims=True)
    blocks = jnp.maximum((total + 255) >> 9, 1)

    def block(b, carried):
        attend_columns(b * BQ, BQ, columns, queries, keys, values, acc, largest_key)
        return carried

    lax.fori_loop(jnp.where(unsafe(shift, square, largest_key), 0, 1), blocks, block, 0)

    @pl.when(total > blocks * BQ)
    def _():
        attend_columns(blocks * BQ, 256, columns, queries, keys, values, acc, largest_key)

    for g in range(GROUPS):
        begin = pl.multiple_of((first_ref[8 * g] >> 7) * 128, 128)
        near = lax.broadcasted_iota(jnp.int32, (WINDOW, OWNERS * SLOTS), 0)
        choose = ones_where(near == pick_ref[g : g + 1, :]).astype(bf16)
        picked = jnp.dot(acc[:, pl.ds(begin, WINDOW)].astype(bf16), choose, preferred_element_type=f32)
        rows[g] = jnp.concatenate((picked, jnp.zeros((128 - HP, OWNERS * SLOTS), f32)), axis=0).T

    def owner(d, carried):
        at = pl.ds(pl.multiple_of(d * SLOTS, 8), SLOTS)
        found = jnp.concatenate([rows[g, at, :] for g in range(GROUPS - 1)], axis=0)
        last = rows[GROUPS - 1, at, :]
        spread = jnp.concatenate([pltpu.roll(last, HD - 40 * i, 1) for i in range(3)], axis=0)
        packed = jnp.where(lanes_below((QROWS, 128), HD), found, spread)
        out_ref[d] = jnp.concatenate((packed, act_ref[d].astype(f32)), axis=0).astype(bf16)
        return carried

    lax.fori_loop(0, OWNERS, owner, 0, unroll=8)


def final_kernel(
    in_ref, slot_ref, home_ref, w_ref, bias_ref, gain_ref, shift_ref, out_ref, attended, acts
):
    shape = (SLOTS, 128)
    for h in range(HEADS):
        for x in range(2):
            whole = in_ref[2 * h + x].astype(f32)
            parts = [pltpu.roll(whole[SLOTS * i : SLOTS * i + SLOTS], 40 * (i + 1), 1) for i in range(3)]
            last = jnp.where(
                lanes_below(shape, 40), parts[0], jnp.where(lanes_below(shape, 80), parts[1], parts[2])
            )
            attended[x * PART : x * PART + PART, h * 128 : h * 128 + 128] = jnp.concatenate(
                (whole[:QROWS], last), axis=0
            ).astype(bf16)
            at = 8 * (2 * h + x)
            for c in range(9):
                acts[at : at + 8, c * 128 : c * 128 + 128] = whole[QROWS + 8 * c : QROWS + 8 * c + 8]
    slot = lax.broadcasted_iota(jnp.int32, (CAP, CAP), 1)
    choose = ones_where(slot == slot_ref[:, 0:1]).astype(bf16)
    listed_rows = jnp.dot(choose, attended[...], preferred_element_type=f32)
    place = lax.broadcasted_iota(jnp.int32, (CAP, BLOCKS * 8), 1)
    home = home_ref[:, 0:1]
    choose = ones_where(place == home).astype(bf16)
    got = acts[...].astype(bf16)
    tokens = jnp.dot(choose, got, preferred_element_type=f32)
    tail = jnp.zeros((CAP, 256), f32)
    rank = home & 7
    for i in range(3):
        there = jnp.where((home >= 0) & (rank >> 1 == i), home - rank + EACH + (rank & 1), -1)
        choose = ones_where(place == there).astype(bf16)
        pair = jnp.concatenate(
            (got[:, i * 128 : i * 128 + 128], got[:, (i + 3) * 128 : (i + 4) * 128]), axis=1
        )
        tail = tail + jnp.dot(choose, pair, preferred_element_type=f32)
    tokens = jnp.concatenate((tokens, tail), axis=1)
    hidden = tokens + bias_ref[...][None]
    low = lanes_below((CAP, 128), HD)
    for p in range(HEADS // 2):
        first = listed_rows[:, p * 256 : p * 256 + 128]
        second = pltpu.roll(listed_rows[:, p * 256 + 128 : p * 256 + 256], HD, 1)
        both = jnp.concatenate((jnp.where(low, first, second), second), axis=1)[:, : 2 * HD]
        hidden = hidden + jnp.dot(
            both.astype(bf16), w_ref[p * 2 * HD : (p + 1) * 2 * HD, :], preferred_element_type=f32
        )
    hidden = hidden.astype(bf16).astype(f32)
    normed = layer_norm(hidden, gain_ref[...][None], shift_ref[...][None])
    out_ref[0] = jnp.where(slot_ref[:, 0:1] >= 0, normed, 0.0).astype(bf16)


def count_before(values):
    place = jnp.arange(values.shape[0])
    earlier = (place[:, None] > place[None, :]).astype(bf16)
    return jnp.dot(earlier, values.astype(bf16), preferred_element_type=f32).astype(jnp.int32)


def routes(mask_tokens, assignment, me_x, me_block):
    blocks, _ = where_tokens(mask_tokens)
    listed = mask_tokens >= 0
    hit = listed[:, :, None] & (blocks[:, :, None] == jnp.arange(BLOCKS)[None, None, :])
    count = jnp.sum(hit.astype(jnp.int32), axis=1)
    odd = (jnp.arange(OWNERS)[:, None] + jnp.arange(BLOCKS)[None, :]) % 2
    held = (count + (odd == me_x)) // 2
    block_total = jnp.sum(held, axis=0)
    first = count_before(jnp.concatenate((block_total, jnp.zeros((8,), jnp.int32))))
    column = first[None, :BLOCKS] + count_before(held)
    column = column.reshape(OWNERS, GROUPS, 8) - (first[0:BLOCKS:8] // 128 * 128)[None, :, None]
    rank = jnp.arange(3)
    pick = jnp.where(
        rank < held.reshape(OWNERS, GROUPS, 8)[..., None], column[..., None] + rank, -1
    ).reshape(OWNERS, GROUPS * SLOTS)
    pick = jnp.take(pick, assignment, axis=0).reshape(OWNERS, GROUPS, SLOTS)
    pick = pick.transpose(1, 0, 2).reshape(GROUPS, OWNERS * SLOTS)

    lists = jnp.take(mask_tokens, assignment, axis=0)
    blocks, local = where_tokens(lists)
    here = (lists >= 0) & (blocks == me_block)
    entry = jnp.arange(CAP)
    earlier = (entry[:, None] < entry[None, :]).astype(bf16)
    order = jnp.dot(here.astype(bf16), earlier, preferred_element_type=f32).astype(jnp.int32)
    hit = here[:, :, None] & (order[:, :, None] == jnp.arange(8)[None, None, :])
    act_pick = jnp.sum(jnp.where(hit, local[:, :, None] + 1, 0), axis=1) - 1

    own = lax.dynamic_index_in_dim(lists, me_block, 0, keepdims=False)
    own_block, _ = where_tokens(own)
    same = (own_block[:, None] == own_block[None, :]) & (own >= 0)[:, None]
    order = jnp.sum((same & (entry[:, None] < entry[None, :])).astype(jnp.int32), axis=0)
    half = (order + own_block + lax.dynamic_index_in_dim(assignment, me_block, 0, keepdims=False)) % 2
    slot = jnp.where(own >= 0, half * PART + own_block * 3 + order // 2, -1)
    home = jnp.where(own >= 0, own_block * 8 + order, -1)
    wide = (CAP, 128)
    return (
        first,
        pick,
        act_pick,
        jnp.broadcast_to(slot[:, None], wide),
        jnp.broadcast_to(home[:, None], wide),
    )


def pack_rows(act_pick, tokens):
    choose = (act_pick[:, :EACH].reshape(OWNERS * EACH, 1) == jnp.arange(TOK)[None, :]).astype(bf16)
    found = jnp.dot(choose, tokens, preferred_element_type=f32).astype(bf16)
    tiles = found.reshape(OWNERS, EACH, 11, 128).transpose(0, 2, 1, 3)
    last = tiles[:, 9:].reshape(OWNERS, EACH, 2, 128)
    last = jnp.concatenate((last, jnp.zeros((OWNERS, 3, 2, 128), bf16)), axis=1)
    return jnp.concatenate((tiles[:, :9], last), axis=2).reshape(OWNERS, QROWS, 128)


def qkv_call(*arrays):
    return pl.pallas_call(
        qkv_kernel,
        in_specs=[pl.BlockSpec(memory_space=pltpu.SMEM)]
        + [vmem()] * 4
        + [pl.BlockSpec(memory_space=pltpu.HBM), vmem()],
        out_specs=vmem(),
        out_shape=jax.ShapeDtypeStruct((2 * HEADS, ROWS, 128), bf16),
        scratch_shapes=[
            pltpu.VMEM((D, 3 * D), bf16),
            pltpu.VMEM((2 * D, 128), f32),
            pltpu.VMEM((2 * D, 128), f32),
            pltpu.VMEM((2, D, 128), f32),
            pltpu.SemaphoreType.DMA((3,)),
        ],
        compiler_params=params(60),
        cost_estimate=pl.CostEstimate(flops=2 * TOK * D * 3 * D, bytes_accessed=14 * MIB, transcendentals=0),
        name="projection",
    )(*arrays)


def attend_call(*arrays):
    return pl.pallas_call(
        attend_kernel,
        in_specs=[pl.BlockSpec(memory_space=pltpu.SMEM), vmem(), vmem(), vmem()],
        out_specs=vmem(),
        out_shape=jax.ShapeDtypeStruct((OWNERS, PACK, 128), bf16),
        scratch_shapes=[
            pltpu.VMEM((TOKENS, 256), bf16),
            pltpu.VMEM((HP, TOKENS), bf16),
            pltpu.VMEM((HD, COLUMNS + 6 * 128), f32),
            pltpu.VMEM((256, BQ), bf16),
            pltpu.VMEM((HP, COLUMNS + WINDOW), f32),
            pltpu.VMEM((GROUPS, OWNERS * SLOTS, 128), f32),
        ],
        compiler_params=params(30),
        cost_estimate=pl.CostEstimate(
            flops=4 * COLUMNS * TOKENS * 256, bytes_accessed=8 * MIB, transcendentals=COLUMNS * TOKENS
        ),
        name="attend",
    )(*arrays)


def finish_call(*arrays):
    return pl.pallas_call(
        final_kernel,
        in_specs=[vmem()] * 7,
        out_specs=vmem(),
        out_shape=jax.ShapeDtypeStruct((1, CAP, D), bf16),
        scratch_shapes=[pltpu.VMEM((CAP, HEADS * 128), bf16), pltpu.VMEM((BLOCKS * 8, 9 * 128), f32)],
        compiler_params=params(30),
        cost_estimate=pl.CostEstimate(flops=2 * TOK * D * D, bytes_accessed=10 * MIB, transcendentals=0),
        name="finish",
    )(*arrays)


def local(
    activations,
    attn_gain,
    attn_shift,
    w_qkv,
    b_qkv,
    w_out,
    b_out,
    final_gain,
    final_shift,
    mask_tokens,
    assignment,
):
    tokens = activations.reshape(TOK, D)
    axes = ("tm", "y", "x")
    me_x = lax.axis_index("x")
    me_block = lax.axis_index("tm") * 8 + lax.axis_index("y") * 2 + me_x

    sent = qkv_call(me_block[None], tokens, attn_gain, attn_shift, mask_tokens, w_qkv, b_qkv)
    arrived = lax.all_to_all(sent, axes, 0, 0, tiled=True)

    first, pick, act_pick, slot, home = routes(mask_tokens, assignment, me_x, me_block)
    act_out = pack_rows(act_pick, tokens)
    first, pick, act_out, slot, home = lax.optimization_barrier((first, pick, act_out, slot, home))
    o_in = lax.all_to_all(attend_call(first, arrived, pick, act_out), axes, 0, 0, tiled=True)
    return finish_call(o_in, slot, home, w_out, b_out, final_gain, final_shift)


def solution(mesh):
    times, spaces, clips = (mesh.shape[a] for a in ("tm", "space", "clip"))
    fine = Mesh(mesh.devices.reshape(times, spaces // 2, 2, clips), ("tm", "y", "x", "clip"))
    in_specs = (
        P(("clip", "tm"), ("y", "x"), None),
        P(),
        P(),
        P(),
        P(),
        P(),
        P(),
        P(),
        P(),
        P("clip", None),
        P("clip"),
    )
    out_specs = P(("clip", "tm", "y", "x"), None, None)
    return jax.shard_map(local, mesh=fine, in_specs=in_specs, out_specs=out_specs, check_vma=False)
```

```python
import functools
import math

import jax
import jax.numpy as jnp
from jax import lax
from jax.experimental import pallas as pl
from jax.experimental.pallas import tpu as pltpu
from jax.sharding import Mesh
from jax.sharding import PartitionSpec as P

EPSILON = 1e-06
D = 1408
HEADS = 16
HD = 88
HP = 96
TOK = 192
MAIN = 128
OWNERS = 32
BLOCKS = 32
CAP = 192
EACH = 6
PART = 96
TOKENS = BLOCKS * TOK
COLUMNS = BLOCKS * PART
QROWS = 72
ROWS = 3 * HD + QROWS
GROUPS = 4
PACK = 2 * QROWS
SLOTS = 24
WINDOW = 8 * PART + 128
BQ = 512
FIRST = 1024
BK = 2048
QK_SCALE = math.log2(math.e) / math.sqrt(HD)
SAFE = 90.0
MIB = 1 << 20

f32 = jnp.float32
bf16 = jnp.bfloat16


def params(vmem_mib):
    return pltpu.CompilerParams(vmem_limit_bytes=vmem_mib * MIB)


def vmem():
    return pl.BlockSpec(memory_space=pltpu.VMEM)


def layer_norm(values, ln_gain, ln_shift):
    centre = jnp.mean(values, axis=-1, keepdims=True)
    deviation = values - centre
    variance = jnp.mean(deviation * deviation, axis=-1, keepdims=True)
    return deviation * lax.rsqrt(variance + EPSILON) * ln_gain + ln_shift


def lanes_below(shape, bound):
    return lax.broadcasted_iota(jnp.int32, shape, 1) < bound


def where_tokens(lists):
    token = jnp.maximum(lists, 0)
    frame, patch = token >> 8, token & 255
    z = (frame * 43) >> 8
    return z * 8 + (patch >> 5), (frame - z * 6) * 32 + (patch & 31)


def ones_where(condition):
    return jnp.where(condition, 1.0, 0.0)


def query_choice(lists, me):
    block, local = where_tokens(lists)
    mine = ones_where((lists >= 0) & (block == me))
    upper = ones_where(
        lax.broadcasted_iota(jnp.int32, (CAP, CAP), 0) < lax.broadcasted_iota(jnp.int32, (CAP, CAP), 1)
    )
    rank = jnp.dot(mine.astype(bf16), upper.astype(bf16), preferred_element_type=f32)
    count = jnp.sum(mine, axis=1, keepdims=True)
    lower = ones_where(
        lax.broadcasted_iota(jnp.int32, (OWNERS, OWNERS), 0)
        > lax.broadcasted_iota(jnp.int32, (OWNERS, OWNERS), 1)
    ).astype(bf16)
    odd = ((lax.broadcasted_iota(jnp.int32, (OWNERS, 1), 0) + me) & 1) == 1
    bases, many, few = [], jnp.zeros_like(count), jnp.zeros_like(count)
    for k in range(0, EACH, 2):
        many, few = many + ones_where(count > k), few + ones_where(count > k + 1)
    for held in (jnp.where(odd, few, many), jnp.where(odd, many, few)):
        held = jnp.broadcast_to(held, (OWNERS, 128)).astype(bf16)
        bases.append(jnp.dot(lower, held, preferred_element_type=f32)[:, 0:1] + len(bases) * PART)
    bases = (jnp.where(odd, bases[1], bases[0]), jnp.where(odd, bases[0], bases[1]))
    lane = lax.broadcasted_iota(jnp.int32, (OWNERS, CAP), 1).astype(f32)
    slots, tokens = [], []
    for k in range(EACH):
        token = jnp.sum(jnp.where(rank == k, mine * local.astype(f32), 0.0), axis=1, keepdims=True)
        have = count > k
        slots.append(ones_where(have & (lane == bases[k % 2] + k // 2)))
        tokens.append(ones_where(have & (lane == token)))
    return lax.dot_general(
        jnp.concatenate(slots, axis=0).astype(bf16),
        jnp.concatenate(tokens, axis=0).astype(bf16),
        (((0,), (0,)), ((), ())),
        preferred_element_type=f32,
    ).astype(bf16)


def qkv_kernel(
    me_ref, x_ref, gain_ref, shift_ref, lists_ref, w_ref, bias_ref, out_ref, buffer, main, rest, asked, sems
):
    copies = [
        pltpu.make_async_copy(w_ref.at[:, pl.ds(at, D)], buffer.at[:, pl.ds(at, D)], sems.at[i])
        for i, at in enumerate((D, 2 * D, 0))
    ]
    for copy in copies:
        copy.start()
    normed = layer_norm(x_ref[...].astype(f32), gain_ref[...][None], shift_ref[...][None]).astype(bf16)
    chosen = jnp.dot(query_choice(lists_ref[...], me_ref[0]), normed, preferred_element_type=f32)
    chosen = chosen.astype(bf16)
    for copy, at, rows in zip(copies, (D, 2 * D, 0), (normed, normed, chosen)):
        copy.wait()
        part = jnp.dot(rows, buffer[:, at : at + D], preferred_element_type=f32)
        part = (part + bias_ref[at : at + D][None]).astype(bf16).astype(f32)
        if at == 0:
            for x in range(2):
                half = part[x * PART : x * PART + PART]
                asked[x] = jnp.concatenate((half, half[:32]), axis=0).T
        else:
            tail = part[MAIN:]
            main[at - D : at, :] = part[:MAIN].T
            rest[at - D : at, :] = jnp.concatenate((tail, tail), axis=0).T
    low = lanes_below((HD, 128), 64)
    queries = lanes_below((QROWS, 128), PART)
    for h in range(HEADS):
        k_rows, v_rows = slice(h * HD, h * HD + HD), slice(D + h * HD, D + h * HD + HD)
        both = jnp.where(low, rest[k_rows, :], rest[v_rows, :])
        for x in range(2):
            top = asked[x, h * HD : h * HD + QROWS, :]
            last = jnp.concatenate(
                (asked[x, h * HD + QROWS : h * HD + HD, :], jnp.zeros((8, 128), f32)), axis=0
            )
            spread = jnp.concatenate((last, pltpu.roll(last, 64, 1), pltpu.roll(last, 32, 1)), axis=0)
            out_ref[2 * h + x] = jnp.concatenate(
                (main[k_rows, :], main[v_rows, :], both, jnp.where(queries, top, spread)), axis=0
            ).astype(bf16)


def unpack_pair(first, second):
    low = lanes_below(first.shape, 64)
    return (
        jnp.where(low, first, pltpu.roll(second, 64, 1)),
        jnp.where(low, pltpu.roll(first, 64, 1), second),
    )


def put_keys(tile, k_tile, v_tile, keys, values):
    at = pl.ds(tile * 128, 128)
    ones = jnp.ones((HP - HD, 128), f32)
    turned = jnp.concatenate((k_tile, ones, jnp.zeros((128 - HP, 128), f32)), axis=0).T.astype(bf16)
    keys[at, 0:128] = turned
    keys[at, 128:256] = turned
    values[:, at] = jnp.concatenate((v_tile, ones), axis=0).astype(bf16)
    return jnp.sum(k_tile * k_tile, axis=0, keepdims=True)


def put_queries(packed, first, count, columns):
    shape = (HD - QROWS, 128)
    parts = [
        pltpu.roll(packed[24 * i : 24 * i + HD - QROWS], 32 * (i + 1), 1) for i in range(3)
    ]
    last = jnp.where(lanes_below(shape, 32), parts[0], jnp.where(lanes_below(shape, 64), parts[1], parts[2]))
    whole = jnp.concatenate((packed, last), axis=0)
    lane = lax.broadcasted_iota(jnp.int32, whole.shape, 1)
    turn = first & 127
    turned = pltpu.roll(jnp.where(lane < count, whole, 0.0), turn, 1)
    at = pl.ds(pl.multiple_of((first >> 7) * 128, 128), 128)
    columns[:, at] = columns[:, at] + jnp.where(lane >= turn, turned, 0.0)
    at = pl.ds(pl.multiple_of((first >> 7) * 128 + 128, 128), 128)
    columns[:, at] = jnp.where(lane < turn, turned, 0.0)


def set_shift(queries, at, shift):
    high = shift.astype(bf16).astype(f32)
    middle = (shift - high).astype(bf16).astype(f32)
    low = shift - high - middle
    row = lax.broadcasted_iota(jnp.int32, (8, shift.shape[1]), 0)
    rows = jnp.where(row == 0, -high, jnp.where(row == 1, -middle, jnp.where(row == 2, -low, 0.0)))
    old = queries[HP - 16 : HP, at].astype(f32)
    queries[HP - 16 : HP, at] = jnp.concatenate((old[:8], rows), axis=0).astype(bf16)


def scores_of(keys, queries, first, count, at):
    return jnp.dot(keys[pl.ds(first, count), :], queries[:, at], preferred_element_type=f32)


def start_columns(at, columns, queries, keys):
    scaled = columns[:, at] * QK_SCALE
    high = scaled.astype(bf16).astype(f32)
    width = scaled.shape[1]
    zeros = jnp.zeros((128 - HD, width), f32)
    here = pl.ds(0, width)
    queries[0:128, here] = jnp.concatenate((high, zeros), axis=0).astype(bf16)
    queries[128:256, here] = jnp.concatenate((scaled - high, zeros), axis=0).astype(bf16)
    shift = jnp.max(scores_of(keys, queries, 0, 128, here), axis=0, keepdims=True)
    set_shift(queries, here, shift)
    return shift, jnp.sum(scaled * scaled, axis=0, keepdims=True)


def unsafe(shift, square, largest_key):
    return jnp.logical_not(jnp.max(jnp.sqrt(square * largest_key) * 1.01 - shift) <= SAFE)


def weigh(keys, queries, values, first, width):
    weights = jnp.exp2(scores_of(keys, queries, first, BK, pl.ds(0, width))).astype(bf16)
    return jnp.dot(values[:, first : first + BK], weights, preferred_element_type=f32)


def attend_columns(start, width, columns, queries, keys, values, acc, largest_key):
    at = pl.ds(pl.multiple_of(start, 256), width)
    here = pl.ds(0, width)
    shift, square = start_columns(at, columns, queries, keys)

    @pl.when(unsafe(shift, square, largest_key))
    def _():
        def step(i, above):
            got = scores_of(keys, queries, pl.multiple_of(i * 256, 256), 256, here)
            return jnp.maximum(above, jnp.max(got, axis=0, keepdims=True))

        above = lax.fori_loop(0, TOKENS // 256, step, jnp.zeros((1, width), f32))
        set_shift(queries, here, shift + above)

    total = weigh(keys, queries, values, 0, width)
    for first in range(BK, TOKENS, BK):
        total = total + weigh(keys, queries, values, first, width)
    acc[:, at] = total / total[HD : HD + 1, :]


def unpack_keys(chunk, in_ref, keys, values):
    largest = jnp.zeros((1, 128), f32)
    for i in range(BLOCKS // 2):
        if chunk < 2:
            block = chunk * (BLOCKS // 2) + i
            k_tile = in_ref[block, 0:96].astype(f32)[:HD]
            v_tile = in_ref[block, 80:176].astype(f32)[8:]
        else:
            rests = [in_ref[2 * i + j, 176:272].astype(f32)[:HD] for j in range(2)]
            k_tile, v_tile = unpack_pair(*rests)
        square = put_keys(chunk * (BLOCKS // 2) + i, k_tile, v_tile, keys, values)
        largest = jnp.maximum(largest, square)
    return largest


def attend_kernel(
    first_ref, in_ref, pick_ref, act_ref, out_ref, keys, values, columns, queries, acc, rows
):
    columns[:, 0:128] = jnp.zeros((HD, 128), f32)

    def place(block, carried):
        first = first_ref[block]
        packed = in_ref[block, 256:336].astype(f32)[8:]
        put_queries(packed, first, first_ref[block + 1] - first, columns)
        return carried

    lax.fori_loop(0, BLOCKS, place, 0, unroll=8)
    total = first_ref[BLOCKS]
    used = (total >> 7) * 128 + 128

    def clear(i, carried):
        columns[:, pl.ds(pl.multiple_of(used + i * 128, 128), 128)] = jnp.zeros((HD, 128), f32)
        return carried

    lax.fori_loop(0, 9, clear, 0)
    acc[...] = jnp.zeros_like(acc)

    largest = unpack_keys(0, in_ref, keys, values)
    shift, square = start_columns(pl.ds(0, FIRST), columns, queries, keys)
    found = weigh(keys, queries, values, 0, FIRST)
    for chunk in (1, 2):
        largest = jnp.maximum(largest, unpack_keys(chunk, in_ref, keys, values))
        found = found + weigh(keys, queries, values, chunk * BK, FIRST)
    acc[:, 0:FIRST] = found / found[HD : HD + 1, :]
    largest_key = jnp.max(largest, axis=1, keepdims=True)
    more = jnp.maximum(total - FIRST, 0)
    blocks = (more + 255) >> 9

    def block(b, carried):
        attend_columns(FIRST + b * BQ, BQ, columns, queries, keys, values, acc, largest_key)
        return carried

    lax.fori_loop(jnp.where(unsafe(shift, square, largest_key), -FIRST // BQ, 0), blocks, block, 0)

    @pl.when(more > blocks * BQ)
    def _():
        attend_columns(FIRST + blocks * BQ, 256, columns, queries, keys, values, acc, largest_key)

    for g in range(GROUPS):
        begin = pl.multiple_of((first_ref[8 * g] >> 7) * 128, 128)
        near = lax.broadcasted_iota(jnp.int32, (WINDOW, OWNERS * SLOTS), 0)
        choose = ones_where(near == pick_ref[g : g + 1, :]).astype(bf16)
        picked = jnp.dot(acc[:, pl.ds(begin, WINDOW)].astype(bf16), choose, preferred_element_type=f32)
        rows[g] = jnp.concatenate((picked, jnp.zeros((128 - HP, OWNERS * SLOTS), f32)), axis=0).T

    def owner(d, carried):
        at = pl.ds(pl.multiple_of(d * SLOTS, 8), SLOTS)
        found = jnp.concatenate([rows[g, at, :] for g in range(GROUPS - 1)], axis=0)
        last = rows[GROUPS - 1, at, :]
        spread = jnp.concatenate([pltpu.roll(last, HD - 40 * i, 1) for i in range(3)], axis=0)
        packed = jnp.where(lanes_below((QROWS, 128), HD), found, spread)
        out_ref[d] = jnp.concatenate((packed, act_ref[d].astype(f32)), axis=0).astype(bf16)
        return carried

    lax.fori_loop(0, OWNERS, owner, 0, unroll=8)


def final_kernel(
    in_ref, slot_ref, home_ref, w_ref, bias_ref, gain_ref, shift_ref, out_ref, attended, acts
):
    shape = (SLOTS, 128)
    for h in range(HEADS):
        for x in range(2):
            whole = in_ref[2 * h + x].astype(f32)
            parts = [pltpu.roll(whole[SLOTS * i : SLOTS * i + SLOTS], 40 * (i + 1), 1) for i in range(3)]
            last = jnp.where(
                lanes_below(shape, 40), parts[0], jnp.where(lanes_below(shape, 80), parts[1], parts[2])
            )
            attended[x * PART : x * PART + PART, h * 128 : h * 128 + 128] = jnp.concatenate(
                (whole[:QROWS], last), axis=0
            ).astype(bf16)
            at = 8 * (2 * h + x)
            for c in range(9):
                acts[at : at + 8, c * 128 : c * 128 + 128] = whole[QROWS + 8 * c : QROWS + 8 * c + 8]
    slot = lax.broadcasted_iota(jnp.int32, (CAP, CAP), 1)
    choose = ones_where(slot == slot_ref[:, 0:1]).astype(bf16)
    listed_rows = jnp.dot(choose, attended[...], preferred_element_type=f32)
    place = lax.broadcasted_iota(jnp.int32, (CAP, BLOCKS * 8), 1)
    home = home_ref[:, 0:1]
    choose = ones_where(place == home).astype(bf16)
    got = acts[...].astype(bf16)
    tokens = jnp.dot(choose, got, preferred_element_type=f32)
    tail = jnp.zeros((CAP, 256), f32)
    rank = home & 7
    for i in range(3):
        there = jnp.where((home >= 0) & (rank >> 1 == i), home - rank + EACH + (rank & 1), -1)
        choose = ones_where(place == there).astype(bf16)
        pair = jnp.concatenate(
            (got[:, i * 128 : i * 128 + 128], got[:, (i + 3) * 128 : (i + 4) * 128]), axis=1
        )
        tail = tail + jnp.dot(choose, pair, preferred_element_type=f32)
    tokens = jnp.concatenate((tokens, tail), axis=1)
    hidden = tokens + bias_ref[...][None]
    low = lanes_below((CAP, 128), HD)
    for p in range(HEADS // 2):
        first = listed_rows[:, p * 256 : p * 256 + 128]
        second = pltpu.roll(listed_rows[:, p * 256 + 128 : p * 256 + 256], HD, 1)
        both = jnp.concatenate((jnp.where(low, first, second), second), axis=1)[:, : 2 * HD]
        hidden = hidden + jnp.dot(
            both.astype(bf16), w_ref[p * 2 * HD : (p + 1) * 2 * HD, :], preferred_element_type=f32
        )
    hidden = hidden.astype(bf16).astype(f32)
    normed = layer_norm(hidden, gain_ref[...][None], shift_ref[...][None])
    out_ref[0] = jnp.where(slot_ref[:, 0:1] >= 0, normed, 0.0).astype(bf16)


def count_before(values):
    place = jnp.arange(values.shape[0])
    earlier = (place[:, None] > place[None, :]).astype(bf16)
    return jnp.dot(earlier, values.astype(bf16), preferred_element_type=f32).astype(jnp.int32)


def routes(mask_tokens, assignment, me_x, me_block):
    blocks, _ = where_tokens(mask_tokens)
    listed = mask_tokens >= 0
    hit = listed[:, :, None] & (blocks[:, :, None] == jnp.arange(BLOCKS)[None, None, :])
    count = jnp.sum(hit.astype(jnp.int32), axis=1)
    odd = (jnp.arange(OWNERS)[:, None] + jnp.arange(BLOCKS)[None, :]) % 2
    held = (count + (odd == me_x)) // 2
    block_total = jnp.sum(held, axis=0)
    first = count_before(jnp.concatenate((block_total, jnp.zeros((8,), jnp.int32))))
    column = first[None, :BLOCKS] + count_before(held)
    column = column.reshape(OWNERS, GROUPS, 8) - (first[0:BLOCKS:8] // 128 * 128)[None, :, None]
    rank = jnp.arange(3)
    pick = jnp.where(
        rank < held.reshape(OWNERS, GROUPS, 8)[..., None], column[..., None] + rank, -1
    ).reshape(OWNERS, GROUPS * SLOTS)
    pick = jnp.take(pick, assignment, axis=0).reshape(OWNERS, GROUPS, SLOTS)
    pick = pick.transpose(1, 0, 2).reshape(GROUPS, OWNERS * SLOTS)

    lists = jnp.take(mask_tokens, assignment, axis=0)
    blocks, local = where_tokens(lists)
    here = (lists >= 0) & (blocks == me_block)
    entry = jnp.arange(CAP)
    earlier = (entry[:, None] < entry[None, :]).astype(bf16)
    order = jnp.dot(here.astype(bf16), earlier, preferred_element_type=f32).astype(jnp.int32)
    hit = here[:, :, None] & (order[:, :, None] == jnp.arange(8)[None, None, :])
    act_pick = jnp.sum(jnp.where(hit, local[:, :, None] + 1, 0), axis=1) - 1

    own = lax.dynamic_index_in_dim(lists, me_block, 0, keepdims=False)
    own_block, _ = where_tokens(own)
    same = (own_block[:, None] == own_block[None, :]) & (own >= 0)[:, None]
    order = jnp.sum((same & (entry[:, None] < entry[None, :])).astype(jnp.int32), axis=0)
    half = (order + own_block + lax.dynamic_index_in_dim(assignment, me_block, 0, keepdims=False)) % 2
    slot = jnp.where(own >= 0, half * PART + own_block * 3 + order // 2, -1)
    home = jnp.where(own >= 0, own_block * 8 + order, -1)
    wide = (CAP, 128)
    return (
        first,
        pick,
        act_pick,
        jnp.broadcast_to(slot[:, None], wide),
        jnp.broadcast_to(home[:, None], wide),
    )


def pack_rows(act_pick, tokens):
    choose = (act_pick[:, :EACH].reshape(OWNERS * EACH, 1) == jnp.arange(TOK)[None, :]).astype(bf16)
    found = jnp.dot(choose, tokens, preferred_element_type=f32).astype(bf16)
    tiles = found.reshape(OWNERS, EACH, 11, 128).transpose(0, 2, 1, 3)
    last = tiles[:, 9:].reshape(OWNERS, EACH, 2, 128)
    last = jnp.concatenate((last, jnp.zeros((OWNERS, 3, 2, 128), bf16)), axis=1)
    return jnp.concatenate((tiles[:, :9], last), axis=2).reshape(OWNERS, QROWS, 128)


def qkv_call(*arrays):
    return pl.pallas_call(
        qkv_kernel,
        in_specs=[pl.BlockSpec(memory_space=pltpu.SMEM)]
        + [vmem()] * 4
        + [pl.BlockSpec(memory_space=pltpu.HBM), vmem()],
        out_specs=vmem(),
        out_shape=jax.ShapeDtypeStruct((2 * HEADS, ROWS, 128), bf16),
        scratch_shapes=[
            pltpu.VMEM((D, 3 * D), bf16),
            pltpu.VMEM((2 * D, 128), f32),
            pltpu.VMEM((2 * D, 128), f32),
            pltpu.VMEM((2, D, 128), f32),
            pltpu.SemaphoreType.DMA((3,)),
        ],
        compiler_params=params(60),
        cost_estimate=pl.CostEstimate(flops=2 * TOK * D * 3 * D, bytes_accessed=14 * MIB, transcendentals=0),
        name="projection",
    )(*arrays)


def attend_call(*arrays):
    return pl.pallas_call(
        attend_kernel,
        in_specs=[pl.BlockSpec(memory_space=pltpu.SMEM), vmem(), vmem(), vmem()],
        out_specs=vmem(),
        out_shape=jax.ShapeDtypeStruct((OWNERS, PACK, 128), bf16),
        scratch_shapes=[
            pltpu.VMEM((TOKENS, 256), bf16),
            pltpu.VMEM((HP, TOKENS), bf16),
            pltpu.VMEM((HD, COLUMNS + 10 * 128), f32),
            pltpu.VMEM((256, FIRST), bf16),
            pltpu.VMEM((HP, COLUMNS + WINDOW), f32),
            pltpu.VMEM((GROUPS, OWNERS * SLOTS, 128), f32),
        ],
        compiler_params=params(44),
        cost_estimate=pl.CostEstimate(
            flops=4 * COLUMNS * TOKENS * 256, bytes_accessed=8 * MIB, transcendentals=COLUMNS * TOKENS
        ),
        name="attend",
    )(*arrays)


def finish_call(*arrays):
    return pl.pallas_call(
        final_kernel,
        in_specs=[vmem()] * 7,
        out_specs=vmem(),
        out_shape=jax.ShapeDtypeStruct((1, CAP, D), bf16),
        scratch_shapes=[pltpu.VMEM((CAP, HEADS * 128), bf16), pltpu.VMEM((BLOCKS * 8, 9 * 128), f32)],
        compiler_params=params(44),
        cost_estimate=pl.CostEstimate(flops=2 * TOK * D * D, bytes_accessed=10 * MIB, transcendentals=0),
        name="finish",
    )(*arrays)


def local(
    activations,
    attn_gain,
    attn_shift,
    w_qkv,
    b_qkv,
    w_out,
    b_out,
    final_gain,
    final_shift,
    mask_tokens,
    assignment,
):
    tokens = activations.reshape(TOK, D)
    axes = ("tm", "y", "x")
    me_x = lax.axis_index("x")
    me_block = lax.axis_index("tm") * 8 + lax.axis_index("y") * 2 + me_x

    sent = qkv_call(me_block[None], tokens, attn_gain, attn_shift, mask_tokens, w_qkv, b_qkv)
    arrived = lax.all_to_all(sent, axes, 0, 0, tiled=True)

    first, pick, act_pick, slot, home = routes(mask_tokens, assignment, me_x, me_block)
    act_out = pack_rows(act_pick, tokens)
    first, pick, act_out, slot, home = lax.optimization_barrier((first, pick, act_out, slot, home))
    o_in = lax.all_to_all(attend_call(first, arrived, pick, act_out), axes, 0, 0, tiled=True)
    return finish_call(o_in, slot, home, w_out, b_out, final_gain, final_shift)


def solution(mesh):
    times, spaces, clips = (mesh.shape[a] for a in ("tm", "space", "clip"))
    fine = Mesh(mesh.devices.reshape(times, spaces // 2, 2, clips), ("tm", "y", "x", "clip"))
    in_specs = (
        P(("clip", "tm"), ("y", "x"), None),
        P(),
        P(),
        P(),
        P(),
        P(),
        P(),
        P(),
        P(),
        P("clip", None),
        P("clip"),
    )
    out_specs = P(("clip", "tm", "y", "x"), None, None)
    return jax.shard_map(local, mesh=fine, in_specs=in_specs, out_specs=out_specs, check_vma=False)
```

```python
import functools
import math

import jax
import jax.numpy as jnp
from jax import lax
from jax.experimental import pallas as pl
from jax.experimental.pallas import tpu as pltpu
from jax.sharding import Mesh
from jax.sharding import PartitionSpec as P

EPSILON = 1e-06
D = 1408
HEADS = 16
HD = 88
HP = 96
TOK = 192
MAIN = 128
OWNERS = 32
BLOCKS = 32
CAP = 192
EACH = 6
PART = 96
TOKENS = BLOCKS * TOK
COLUMNS = BLOCKS * PART
QROWS = 72
ROWS = 3 * HD + QROWS
GROUPS = 4
PACK = 2 * QROWS
SLOTS = 24
WINDOW = 8 * PART + 128
BQ = 512
BK = 2048
QK_SCALE = math.log2(math.e) / math.sqrt(HD)
SAFE = 90.0
MIB = 1 << 20

f32 = jnp.float32
bf16 = jnp.bfloat16


def params(vmem_mib):
    return pltpu.CompilerParams(vmem_limit_bytes=vmem_mib * MIB)


def vmem():
    return pl.BlockSpec(memory_space=pltpu.VMEM)


def layer_norm(values, ln_gain, ln_shift):
    centre = jnp.mean(values, axis=-1, keepdims=True)
    deviation = values - centre
    variance = jnp.mean(deviation * deviation, axis=-1, keepdims=True)
    return deviation * lax.rsqrt(variance + EPSILON) * ln_gain + ln_shift


def lanes_below(shape, bound):
    return lax.broadcasted_iota(jnp.int32, shape, 1) < bound


def block_number(z, y, x):
    return x * 16 + y * 4 + z


def where_tokens(lists):
    token = jnp.maximum(lists, 0)
    frame, patch = token >> 8, token & 255
    z = (frame * 43) >> 8
    return block_number(z, patch >> 6, (patch >> 5) & 1), (frame - z * 6) * 32 + (patch & 31)


def ones_where(condition):
    return jnp.where(condition, 1.0, 0.0)


def query_choice(lists, me):
    block, local = where_tokens(lists)
    mine = ones_where((lists >= 0) & (block == me))
    upper = ones_where(
        lax.broadcasted_iota(jnp.int32, (CAP, CAP), 0) < lax.broadcasted_iota(jnp.int32, (CAP, CAP), 1)
    )
    rank = jnp.dot(mine.astype(bf16), upper.astype(bf16), preferred_element_type=f32)
    count = jnp.sum(mine, axis=1, keepdims=True)
    lower = ones_where(
        lax.broadcasted_iota(jnp.int32, (OWNERS, OWNERS), 0)
        > lax.broadcasted_iota(jnp.int32, (OWNERS, OWNERS), 1)
    ).astype(bf16)
    odd = ((lax.broadcasted_iota(jnp.int32, (OWNERS, 1), 0) + me) & 1) == 1
    bases, many, few = [], jnp.zeros_like(count), jnp.zeros_like(count)
    for k in range(0, EACH, 2):
        many, few = many + ones_where(count > k), few + ones_where(count > k + 1)
    for held in (jnp.where(odd, few, many), jnp.where(odd, many, few)):
        held = jnp.broadcast_to(held, (OWNERS, 128)).astype(bf16)
        bases.append(jnp.dot(lower, held, preferred_element_type=f32)[:, 0:1] + len(bases) * PART)
    bases = (jnp.where(odd, bases[1], bases[0]), jnp.where(odd, bases[0], bases[1]))
    lane = lax.broadcasted_iota(jnp.int32, (OWNERS, CAP), 1).astype(f32)
    slots, tokens = [], []
    for k in range(EACH):
        token = jnp.sum(jnp.where(rank == k, mine * local.astype(f32), 0.0), axis=1, keepdims=True)
        have = count > k
        slots.append(ones_where(have & (lane == bases[k % 2] + k // 2)))
        tokens.append(ones_where(have & (lane == token)))
    return lax.dot_general(
        jnp.concatenate(slots, axis=0).astype(bf16),
        jnp.concatenate(tokens, axis=0).astype(bf16),
        (((0,), (0,)), ((), ())),
        preferred_element_type=f32,
    ).astype(bf16)


def qkv_kernel(
    me_ref, x_ref, gain_ref, shift_ref, lists_ref, w_ref, bias_ref, out_ref, buffer, main, rest, asked, sems
):
    copies = [
        pltpu.make_async_copy(w_ref.at[:, pl.ds(at, D)], buffer.at[:, pl.ds(at, D)], sems.at[i])
        for i, at in enumerate((D, 2 * D, 0))
    ]
    for copy in copies:
        copy.start()
    normed = layer_norm(x_ref[...].astype(f32), gain_ref[...][None], shift_ref[...][None]).astype(bf16)
    chosen = jnp.dot(query_choice(lists_ref[...], me_ref[0]), normed, preferred_element_type=f32)
    chosen = chosen.astype(bf16)
    for copy, at, rows in zip(copies, (D, 2 * D, 0), (normed, normed, chosen)):
        copy.wait()
        part = jnp.dot(rows, buffer[:, at : at + D], preferred_element_type=f32)
        part = (part + bias_ref[at : at + D][None]).astype(bf16).astype(f32)
        if at == 0:
            for x in range(2):
                half = part[x * PART : x * PART + PART]
                asked[x] = jnp.concatenate((half, half[:32]), axis=0).T
        else:
            tail = part[MAIN:]
            main[at - D : at, :] = part[:MAIN].T
            rest[at - D : at, :] = jnp.concatenate((tail, tail), axis=0).T
    low = lanes_below((HD, 128), 64)
    queries = lanes_below((QROWS, 128), PART)
    for h in range(HEADS):
        k_rows, v_rows = slice(h * HD, h * HD + HD), slice(D + h * HD, D + h * HD + HD)
        both = jnp.where(low, rest[k_rows, :], rest[v_rows, :])
        for x in range(2):
            top = asked[x, h * HD : h * HD + QROWS, :]
            last = jnp.concatenate(
                (asked[x, h * HD + QROWS : h * HD + HD, :], jnp.zeros((8, 128), f32)), axis=0
            )
            spread = jnp.concatenate((last, pltpu.roll(last, 64, 1), pltpu.roll(last, 32, 1)), axis=0)
            out_ref[block_number(h // 4, h % 4, x)] = jnp.concatenate(
                (main[k_rows, :], main[v_rows, :], both, jnp.where(queries, top, spread)), axis=0
            ).astype(bf16)


def unpack_pair(first, second):
    low = lanes_below(first.shape, 64)
    return (
        jnp.where(low, first, pltpu.roll(second, 64, 1)),
        jnp.where(low, pltpu.roll(first, 64, 1), second),
    )


def put_keys(tile, k_tile, v_tile, keys, values):
    at = pl.ds(tile * 128, 128)
    ones = jnp.ones((HP - HD, 128), f32)
    turned = jnp.concatenate((k_tile, ones, jnp.zeros((128 - HP, 128), f32)), axis=0).T.astype(bf16)
    keys[at, 0:128] = turned
    keys[at, 128:256] = turned
    values[:, at] = jnp.concatenate((v_tile, ones), axis=0).astype(bf16)
    return jnp.sum(k_tile * k_tile, axis=0, keepdims=True)


def put_queries(packed, first, count, columns):
    shape = (HD - QROWS, 128)
    parts = [
        pltpu.roll(packed[24 * i : 24 * i + HD - QROWS], 32 * (i + 1), 1) for i in range(3)
    ]
    last = jnp.where(lanes_below(shape, 32), parts[0], jnp.where(lanes_below(shape, 64), parts[1], parts[2]))
    whole = jnp.concatenate((packed, last), axis=0)
    lane = lax.broadcasted_iota(jnp.int32, whole.shape, 1)
    turn = first & 127
    turned = pltpu.roll(jnp.where(lane < count, whole, 0.0), turn, 1)
    at = pl.ds(pl.multiple_of((first >> 7) * 128, 128), 128)
    columns[:, at] = columns[:, at] + jnp.where(lane >= turn, turned, 0.0)
    at = pl.ds(pl.multiple_of((first >> 7) * 128 + 128, 128), 128)
    columns[:, at] = jnp.where(lane < turn, turned, 0.0)


def set_shift(queries, at, shift):
    high = shift.astype(bf16).astype(f32)
    middle = (shift - high).astype(bf16).astype(f32)
    low = shift - high - middle
    row = lax.broadcasted_iota(jnp.int32, (8, shift.shape[1]), 0)
    rows = jnp.where(row == 0, -high, jnp.where(row == 1, -middle, jnp.where(row == 2, -low, 0.0)))
    old = queries[HP - 16 : HP, at].astype(f32)
    queries[HP - 16 : HP, at] = jnp.concatenate((old[:8], rows), axis=0).astype(bf16)


def scores_of(keys, queries, first, count, at):
    return jnp.dot(keys[pl.ds(first, count), :], queries[:, at], preferred_element_type=f32)


def start_columns(at, columns, queries, keys):
    scaled = columns[:, at] * QK_SCALE
    high = scaled.astype(bf16).astype(f32)
    width = scaled.shape[1]
    zeros = jnp.zeros((128 - HD, width), f32)
    here = pl.ds(0, width)
    queries[0:128, here] = jnp.concatenate((high, zeros), axis=0).astype(bf16)
    queries[128:256, here] = jnp.concatenate((scaled - high, zeros), axis=0).astype(bf16)
    shift = jnp.max(scores_of(keys, queries, 0, 128, here), axis=0, keepdims=True)
    set_shift(queries, here, shift)
    return shift, jnp.sum(scaled * scaled, axis=0, keepdims=True)


def unsafe(shift, square, largest_key):
    return jnp.logical_not(jnp.max(jnp.sqrt(square * largest_key) * 1.01 - shift) <= SAFE)


def weigh(keys, queries, values, first, width):
    weights = jnp.exp2(scores_of(keys, queries, first, BK, pl.ds(0, width))).astype(bf16)
    return jnp.dot(values[:, first : first + BK], weights, preferred_element_type=f32)


def attend_columns(start, width, columns, queries, keys, values, acc, largest_key):
    at = pl.ds(pl.multiple_of(start, 256), width)
    here = pl.ds(0, width)
    shift, square = start_columns(at, columns, queries, keys)

    @pl.when(unsafe(shift, square, largest_key))
    def _():
        def step(i, above):
            got = scores_of(keys, queries, pl.multiple_of(i * 256, 256), 256, here)
            return jnp.maximum(above, jnp.max(got, axis=0, keepdims=True))

        above = lax.fori_loop(0, TOKENS // 256, step, jnp.zeros((1, width), f32))
        set_shift(queries, here, shift + above)

    total = weigh(keys, queries, values, 0, width)
    for first in range(BK, TOKENS, BK):
        total = total + weigh(keys, queries, values, first, width)
    acc[:, at] = total / total[HD : HD + 1, :]


def unpack_keys(chunk, in_ref, keys, values):
    largest = jnp.zeros((1, 128), f32)
    for i in range(BLOCKS // 2):
        if chunk < 2:
            block = chunk * (BLOCKS // 2) + i
            k_tile = in_ref[block, 0:96].astype(f32)[:HD]
            v_tile = in_ref[block, 80:176].astype(f32)[8:]
        else:
            rests = [in_ref[2 * i + j, 176:272].astype(f32)[:HD] for j in range(2)]
            k_tile, v_tile = unpack_pair(*rests)
        square = put_keys(chunk * (BLOCKS // 2) + i, k_tile, v_tile, keys, values)
        largest = jnp.maximum(largest, square)
    return largest


def attend_kernel(
    first_ref, in_ref, pick_ref, act_ref, out_ref, keys, values, columns, queries, acc, rows
):
    columns[:, 0:128] = jnp.zeros((HD, 128), f32)

    def place(block, carried):
        first = first_ref[block]
        packed = in_ref[block, 256:336].astype(f32)[8:]
        put_queries(packed, first, first_ref[block + 1] - first, columns)
        return carried

    lax.fori_loop(0, BLOCKS, place, 0, unroll=8)
    total = first_ref[BLOCKS]
    used = (total >> 7) * 128 + 128

    def clear(i, carried):
        columns[:, pl.ds(pl.multiple_of(used + i * 128, 128), 128)] = jnp.zeros((HD, 128), f32)
        return carried

    lax.fori_loop(0, 4, clear, 0)
    acc[...] = jnp.zeros_like(acc)

    largest = unpack_keys(0, in_ref, keys, values)
    shift, square = start_columns(pl.ds(0, BQ), columns, queries, keys)
    found = weigh(keys, queries, values, 0, BQ)
    for chunk in (1, 2):
        largest = jnp.maximum(largest, unpack_keys(chunk, in_ref, keys, values))
        found = found + weigh(keys, queries, values, chunk * BK, BQ)
    acc[:, 0:BQ] = found / found[HD : HD + 1, :]
    largest_key = jnp.max(largest, axis=1, keepdims=True)
    blocks = jnp.maximum((total + 255) >> 9, 1)

    def block(b, carried):
        attend_columns(b * BQ, BQ, columns, queries, keys, values, acc, largest_key)
        return carried

    lax.fori_loop(jnp.where(unsafe(shift, square, largest_key), 0, 1), blocks, block, 0)

    @pl.when(total > blocks * BQ)
    def _():
        attend_columns(blocks * BQ, 256, columns, queries, keys, values, acc, largest_key)

    for g in range(GROUPS):
        begin = pl.multiple_of((first_ref[8 * g] >> 7) * 128, 128)
        near = lax.broadcasted_iota(jnp.int32, (WINDOW, OWNERS * SLOTS), 0)
        choose = ones_where(near == pick_ref[g : g + 1, :]).astype(bf16)
        picked = jnp.dot(acc[:, pl.ds(begin, WINDOW)].astype(bf16), choose, preferred_element_type=f32)
        rows[g] = jnp.concatenate((picked, jnp.zeros((128 - HP, OWNERS * SLOTS), f32)), axis=0).T

    def owner(d, carried):
        at = pl.ds(pl.multiple_of(d * SLOTS, 8), SLOTS)
        found = jnp.concatenate([rows[g, at, :] for g in range(GROUPS - 1)], axis=0)
        last = rows[GROUPS - 1, at, :]
        spread = jnp.concatenate([pltpu.roll(last, HD - 40 * i, 1) for i in range(3)], axis=0)
        packed = jnp.where(lanes_below((QROWS, 128), HD), found, spread)
        out_ref[d] = jnp.concatenate((packed, act_ref[d].astype(f32)), axis=0).astype(bf16)
        return carried

    lax.fori_loop(0, OWNERS, owner, 0, unroll=8)


def final_kernel(
    in_ref, slot_ref, home_ref, w_ref, bias_ref, gain_ref, shift_ref, out_ref, attended, acts
):
    shape = (SLOTS, 128)
    for h in range(HEADS):
        for x in range(2):
            whole = in_ref[2 * h + x].astype(f32)
            parts = [pltpu.roll(whole[SLOTS * i : SLOTS * i + SLOTS], 40 * (i + 1), 1) for i in range(3)]
            last = jnp.where(
                lanes_below(shape, 40), parts[0], jnp.where(lanes_below(shape, 80), parts[1], parts[2])
            )
            attended[x * PART : x * PART + PART, h * 128 : h * 128 + 128] = jnp.concatenate(
                (whole[:QROWS], last), axis=0
            ).astype(bf16)
            at = 8 * (2 * h + x)
            for c in range(9):
                acts[at : at + 8, c * 128 : c * 128 + 128] = whole[QROWS + 8 * c : QROWS + 8 * c + 8]
    slot = lax.broadcasted_iota(jnp.int32, (CAP, CAP), 1)
    choose = ones_where(slot == slot_ref[:, 0:1]).astype(bf16)
    listed_rows = jnp.dot(choose, attended[...], preferred_element_type=f32)
    place = lax.broadcasted_iota(jnp.int32, (CAP, BLOCKS * 8), 1)
    home = home_ref[:, 0:1]
    choose = ones_where(place == home).astype(bf16)
    got = acts[...].astype(bf16)
    tokens = jnp.dot(choose, got, preferred_element_type=f32)
    tail = jnp.zeros((CAP, 256), f32)
    rank = home & 7
    for i in range(3):
        there = jnp.where((home >= 0) & (rank >> 1 == i), home - rank + EACH + (rank & 1), -1)
        choose = ones_where(place == there).astype(bf16)
        pair = jnp.concatenate(
            (got[:, i * 128 : i * 128 + 128], got[:, (i + 3) * 128 : (i + 4) * 128]), axis=1
        )
        tail = tail + jnp.dot(choose, pair, preferred_element_type=f32)
    tokens = jnp.concatenate((tokens, tail), axis=1)
    hidden = tokens + bias_ref[...][None]
    low = lanes_below((CAP, 128), HD)
    for p in range(HEADS // 2):
        first = listed_rows[:, p * 256 : p * 256 + 128]
        second = pltpu.roll(listed_rows[:, p * 256 + 128 : p * 256 + 256], HD, 1)
        both = jnp.concatenate((jnp.where(low, first, second), second), axis=1)[:, : 2 * HD]
        hidden = hidden + jnp.dot(
            both.astype(bf16), w_ref[p * 2 * HD : (p + 1) * 2 * HD, :], preferred_element_type=f32
        )
    hidden = hidden.astype(bf16).astype(f32)
    normed = layer_norm(hidden, gain_ref[...][None], shift_ref[...][None])
    out_ref[0] = jnp.where(slot_ref[:, 0:1] >= 0, normed, 0.0).astype(bf16)


def count_before(values):
    place = jnp.arange(values.shape[0])
    earlier = (place[:, None] > place[None, :]).astype(bf16)
    return jnp.dot(earlier, values.astype(bf16), preferred_element_type=f32).astype(jnp.int32)


def routes(mask_tokens, assignment, me_x, me_block, me_owner):
    blocks, _ = where_tokens(mask_tokens)
    listed = mask_tokens >= 0
    hit = listed[:, :, None] & (blocks[:, :, None] == jnp.arange(BLOCKS)[None, None, :])
    count = jnp.sum(hit.astype(jnp.int32), axis=1)
    odd = (jnp.arange(OWNERS)[:, None] + jnp.arange(BLOCKS)[None, :]) % 2
    held = (count + (odd == me_x)) // 2
    block_total = jnp.sum(held, axis=0)
    first = count_before(jnp.concatenate((block_total, jnp.zeros((8,), jnp.int32))))
    column = first[None, :BLOCKS] + count_before(held)
    column = column.reshape(OWNERS, GROUPS, 8) - (first[0:BLOCKS:8] // 128 * 128)[None, :, None]
    rank = jnp.arange(3)
    pick = jnp.where(
        rank < held.reshape(OWNERS, GROUPS, 8)[..., None], column[..., None] + rank, -1
    ).reshape(OWNERS, GROUPS * SLOTS)
    pick = jnp.take(pick, assignment, axis=0).reshape(OWNERS, GROUPS, SLOTS)
    pick = pick.transpose(1, 0, 2).reshape(GROUPS, OWNERS * SLOTS)

    lists = jnp.take(mask_tokens, assignment, axis=0)
    blocks, local = where_tokens(lists)
    here = (lists >= 0) & (blocks == me_block)
    entry = jnp.arange(CAP)
    earlier = (entry[:, None] < entry[None, :]).astype(bf16)
    order = jnp.dot(here.astype(bf16), earlier, preferred_element_type=f32).astype(jnp.int32)
    hit = here[:, :, None] & (order[:, :, None] == jnp.arange(8)[None, None, :])
    act_pick = jnp.sum(jnp.where(hit, local[:, :, None] + 1, 0), axis=1) - 1

    own = lax.dynamic_index_in_dim(lists, me_owner, 0, keepdims=False)
    own_block, _ = where_tokens(own)
    same = (own_block[:, None] == own_block[None, :]) & (own >= 0)[:, None]
    order = jnp.sum((same & (entry[:, None] < entry[None, :])).astype(jnp.int32), axis=0)
    half = (order + own_block + lax.dynamic_index_in_dim(assignment, me_owner, 0, keepdims=False)) % 2
    slot = jnp.where(own >= 0, half * PART + own_block * 3 + order // 2, -1)
    sender = (own_block & 3) * 8 + ((own_block >> 2) & 3) * 2 + (own_block >> 4)
    home = jnp.where(own >= 0, sender * 8 + order, -1)
    wide = (CAP, 128)
    return (
        first,
        pick,
        act_pick,
        jnp.broadcast_to(slot[:, None], wide),
        jnp.broadcast_to(home[:, None], wide),
    )


def pack_rows(act_pick, tokens):
    choose = (act_pick[:, :EACH].reshape(OWNERS * EACH, 1) == jnp.arange(TOK)[None, :]).astype(bf16)
    found = jnp.dot(choose, tokens, preferred_element_type=f32).astype(bf16)
    tiles = found.reshape(OWNERS, EACH, 11, 128).transpose(0, 2, 1, 3)
    last = tiles[:, 9:].reshape(OWNERS, EACH, 2, 128)
    last = jnp.concatenate((last, jnp.zeros((OWNERS, 3, 2, 128), bf16)), axis=1)
    return jnp.concatenate((tiles[:, :9], last), axis=2).reshape(OWNERS, QROWS, 128)


def qkv_call(*arrays):
    return pl.pallas_call(
        qkv_kernel,
        in_specs=[pl.BlockSpec(memory_space=pltpu.SMEM)]
        + [vmem()] * 4
        + [pl.BlockSpec(memory_space=pltpu.HBM), vmem()],
        out_specs=vmem(),
        out_shape=jax.ShapeDtypeStruct((2 * HEADS, ROWS, 128), bf16),
        scratch_shapes=[
            pltpu.VMEM((D, 3 * D), bf16),
            pltpu.VMEM((2 * D, 128), f32),
            pltpu.VMEM((2 * D, 128), f32),
            pltpu.VMEM((2, D, 128), f32),
            pltpu.SemaphoreType.DMA((3,)),
        ],
        compiler_params=params(60),
        cost_estimate=pl.CostEstimate(flops=2 * TOK * D * 3 * D, bytes_accessed=14 * MIB, transcendentals=0),
        name="projection",
    )(*arrays)


def attend_call(*arrays):
    return pl.pallas_call(
        attend_kernel,
        in_specs=[pl.BlockSpec(memory_space=pltpu.SMEM), vmem(), vmem(), vmem()],
        out_specs=vmem(),
        out_shape=jax.ShapeDtypeStruct((OWNERS, PACK, 128), bf16),
        scratch_shapes=[
            pltpu.VMEM((TOKENS, 256), bf16),
            pltpu.VMEM((HP, TOKENS), bf16),
            pltpu.VMEM((HD, COLUMNS + 6 * 128), f32),
            pltpu.VMEM((256, BQ), bf16),
            pltpu.VMEM((HP, COLUMNS + WINDOW), f32),
            pltpu.VMEM((GROUPS, OWNERS * SLOTS, 128), f32),
        ],
        compiler_params=params(30),
        cost_estimate=pl.CostEstimate(
            flops=4 * COLUMNS * TOKENS * 256, bytes_accessed=8 * MIB, transcendentals=COLUMNS * TOKENS
        ),
        name="attend",
    )(*arrays)


def finish_call(*arrays):
    return pl.pallas_call(
        final_kernel,
        in_specs=[vmem()] * 7,
        out_specs=vmem(),
        out_shape=jax.ShapeDtypeStruct((1, CAP, D), bf16),
        scratch_shapes=[pltpu.VMEM((CAP, HEADS * 128), bf16), pltpu.VMEM((BLOCKS * 8, 9 * 128), f32)],
        compiler_params=params(30),
        cost_estimate=pl.CostEstimate(flops=2 * TOK * D * D, bytes_accessed=10 * MIB, transcendentals=0),
        name="finish",
    )(*arrays)


def local(
    activations,
    attn_gain,
    attn_shift,
    w_qkv,
    b_qkv,
    w_out,
    b_out,
    final_gain,
    final_shift,
    mask_tokens,
    assignment,
):
    tokens = activations.reshape(TOK, D)
    axes = ("tm", "y", "x")
    me_x = lax.axis_index("x")
    me_block = block_number(lax.axis_index("tm"), lax.axis_index("y"), me_x)
    me_owner = lax.axis_index("tm") * 8 + lax.axis_index("y") * 2 + me_x

    sent = qkv_call(me_block[None], tokens, attn_gain, attn_shift, mask_tokens, w_qkv, b_qkv)
    arrived = lax.all_to_all(sent, ("x", "y", "tm"), 0, 0, tiled=True)

    first, pick, act_pick, slot, home = routes(mask_tokens, assignment, me_x, me_block, me_owner)
    act_out = pack_rows(act_pick, tokens)
    first, pick, act_out, slot, home = lax.optimization_barrier((first, pick, act_out, slot, home))
    o_in = lax.all_to_all(attend_call(first, arrived, pick, act_out), axes, 0, 0, tiled=True)
    return finish_call(o_in, slot, home, w_out, b_out, final_gain, final_shift)


def solution(mesh):
    times, spaces, clips = (mesh.shape[a] for a in ("tm", "space", "clip"))
    fine = Mesh(mesh.devices.reshape(times, spaces // 2, 2, clips), ("tm", "y", "x", "clip"))
    in_specs = (
        P(("clip", "tm"), ("y", "x"), None),
        P(),
        P(),
        P(),
        P(),
        P(),
        P(),
        P(),
        P(),
        P("clip", None),
        P("clip"),
    )
    out_specs = P(("clip", "tm", "y", "x"), None, None)
    return jax.shard_map(local, mesh=fine, in_specs=in_specs, out_specs=out_specs, check_vma=False)
```
